512 devices in a mesh: gx: 8 (over x, core), gy: 4 (over y), gz: 16 (over z).
Axes of the slice: x: 4, y: 4, z: 16, core: 2. Of those that a mesh axis runs over, the one named last changes fastest.
Arguments:
- positions: float32 [16, 4, 16, 3, 128], P('gx', 'gy', 'gz'), may hold values from 0 to 11, as said below
- polarity: float32 [16, 4, 16, 128], P('gx', 'gy', 'gz'), may hold values from 0.3 to 2.5
- perm_field: float32 [16, 4, 16, 3, 128], P('gx', 'gy', 'gz'), may hold values from -6 to 6
- groups: int32 [16, 4, 16, 128], P('gx', 'gy', 'gz'), may hold values from 0 to 7
- occupancy: int32 [16, 4, 16], P('gx', 'gy', 'gz'), may hold values from 64 to 128, as said below
Outputs:
- dipoles: float32 [16, 4, 16, 3, 128], P('gx', 'gy', 'gz')
- residual: float32 [16, 4, 16, 3, 128], P('gx', 'gy', 'gz')
The draws below stay inside these ranges and needn't reach their ends.
Inputs may be any that keep to these rules, and one draw needn't show every extreme that they name: `positions`: coordinates lie inside the atom's cell of edge 11; any two atoms of the box are at least 0.6 apart, across cell faces too. `occupancy`: some cells in every draw hold all 128 slots live; dead slots come last in a cell.
All inputs are finite; a program needn't handle non-finite values.
Results may differ from the reference program's by a relative error of at most 0.00035.
Values sent between devices are 32-bit elements; how exact they have to be, the bound alone decides.
A program may use at most 64 MiB of HBM per device.

```python
import functools
import math
import jax
import jax.numpy as jnp
import numpy as np
from jax import lax

CL = 128
ITERS = 3
NX = 16
NY = 4
NZ = 16


CELL_EDGE = 11.0


def shuffled(seed_key):
    return jax.random.permutation(seed_key, CL)


def draw_positions(key, part):
    key = jax.random.fold_in(key, 11)
    cell_count = NX * NY * NZ
    layers = CL // 16
    slot_index = jnp.arange(CL, dtype=jnp.int32)
    lattice = jnp.stack([slot_index // (4 * layers), slot_index // layers % 4, slot_index % layers]).astype(jnp.float32)
    spacing = jnp.array([CELL_EDGE / 4.0, CELL_EDGE / 4.0, CELL_EDGE / layers], jnp.float32)
    order_keys = jax.random.split(jax.random.fold_in(key, 1), cell_count)
    orders = jax.vmap(shuffled)(order_keys)
    placed = jnp.take(lattice, orders, axis=1)
    jitter = jax.random.uniform(jax.random.fold_in(key, 2), (3, cell_count, CL), jnp.float32, -0.25, 0.25)
    coords = (placed + 0.5 + jitter) * spacing[:, None, None]
    return jnp.transpose(coords, (1, 0, 2)).reshape(NX, NY, NZ, 3, CL)


def draw_occupancy(key, part):
    key = jax.random.fold_in(key, 23)
    counts = jax.random.randint(key, (NX, NY, NZ), CL // 2, CL + 1)
    dense_plane = (jnp.arange(NX) % 4 == 0)[:, None, None]
    return jnp.where(dense_plane, CL, counts).astype(jnp.int32)


def set_ends(entries, rng, smallest, largest):
    longest = entries.shape.index(max(entries.shape))
    spots = []
    for shift in (0, 1):
        where = [jax.random.randint(jax.random.fold_in(rng, axis), (), 0, length) for axis, length in enumerate(entries.shape)]
        where[longest] = (where[longest] + shift) % entries.shape[longest]
        spots.append(tuple(where))
    return entries.at[spots[0]].set(smallest).at[spots[1]].set(largest)


def steps_of(own_key, shape, cuts, least, high):
    loudness = 1.0
    for axis_at, parts in cuts:
        steps = jax.random.uniform(jax.random.fold_in(jax.random.fold_in(own_key, 6), axis_at), (parts,), jnp.float32, least / len(cuts), high / len(cuts))
        loudness = loudness * jnp.repeat(jnp.exp(steps), shape[axis_at] // parts).reshape((-1,) + (1,) * (len(shape) - 1 - axis_at))
    return loudness


def scatter_about(own_key, dims, scale, limit, pieces=(), kind=jnp.bfloat16):
    values = scale * jax.random.normal(own_key, dims, jnp.float32)
    if pieces:
        values = values * steps_of(own_key, dims, pieces, -0.22, 0.18)
    return jnp.clip(values, -limit, limit).astype(kind)


def setup_inputs(seed: int = 0) -> dict:
    keys = jax.random.split(jax.random.key(seed), 6)
    return {
        "positions": draw_positions(jax.random.fold_in(keys[5], 71), 0),
        "polarity": jnp.clip(jnp.exp(math.log(2.5) - 2.1202635 * jax.random.uniform(keys[1], (NX, NY, NZ, CL), jnp.float32) ** steps_of(keys[1], (NX, NY, NZ, CL), ((0, 8), (1, 4), (2, 16)), -0.2, 0.2)), 0.3, 2.5),
        "perm_field": scatter_about(keys[2], (NX, NY, NZ, 3, CL), 1.0, 6.0, ((0, 8), (1, 4), (2, 16)), jnp.float32),
        "groups": set_ends(jax.random.randint(keys[3], (NX, NY, NZ, CL), 0, 8), jax.random.fold_in(keys[3], 1), 0, 7).astype(jnp.int32),
        "occupancy": draw_occupancy(jax.random.fold_in(keys[5], 71), 0),
    }


CELL_EDGE = 11.0
CUTOFF = 9.0
THOLE_A = 0.39
EDGE_PICKS = ((-1, 1, 0), (0, -1, 1), (1, 0, -1))

def offset_table(leading_only):
    offsets_list = []
    for offset_x in (-1, 0, 1):
        for offset_y in (-1, 0, 1):
            for offset_z in (-1, 0, 1):
                triple = (offset_x, offset_y, offset_z)
                if triple == (0, 0, 0):
                    continue
                total = offset_x + offset_y + offset_z
                if leading_only and (not (total > 0 or (total == 0 and triple in EDGE_PICKS))):
                    continue
                offsets_list.append(triple)
    return np.array(offsets_list, dtype=np.int32)

def coupling(separation, polar_home, polar_other, weight, on_diagonal):
    squared = lax.optimization_barrier(jnp.sum(separation * separation, axis=-3))
    if on_diagonal:
        squared = squared + jnp.eye(squared.shape[-1], dtype=jnp.float32)
    distance = jnp.sqrt(squared)
    inverse = 1.0 / distance
    inverse_cube = inverse * inverse * inverse
    damping = THOLE_A * squared * distance / jnp.sqrt(polar_home[..., :, None] * polar_other[..., None, :])
    falloff = jnp.exp(-damping)
    screen_three = 1.0 - falloff
    screen_five = 1.0 - (1.0 + damping) * falloff
    tapering = jnp.square(jnp.maximum(1.0 - squared / (CUTOFF * CUTOFF), 0.0))
    factor = tapering * weight
    return (factor * screen_three * inverse_cube, 3.0 * factor * screen_five * inverse_cube * inverse * inverse)

def field_home(separation, coupling_three, coupling_five, source_other):
    project = lax.optimization_barrier(jnp.sum(separation * source_other[..., :, None, :], axis=-3))
    radial = lax.optimization_barrier(jnp.sum(coupling_five[..., None, :, :] * project[..., None, :, :] * separation, axis=-1))
    return radial - lax.optimization_barrier(jnp.sum(coupling_three[..., None, :, :] * source_other[..., :, None, :], axis=-1))

def field_other(separation, coupling_three, coupling_five, source_home):
    project = lax.optimization_barrier(jnp.sum(separation * source_home[..., :, :, None], axis=-3))
    radial = lax.optimization_barrier(jnp.sum(coupling_five[..., None, :, :] * project[..., None, :, :] * separation, axis=-2))
    return radial - lax.optimization_barrier(jnp.sum(coupling_three[..., None, :, :] * source_home[..., :, :, None], axis=-2))

def self_slab(inputs):
    where_slab, polar_slab, source_slab, group_slab = inputs
    separation = where_slab[..., None, :] - where_slab[..., :, None]
    weight = (group_slab[..., :, None] != group_slab[..., None, :]).astype(jnp.float32)
    coupling_three, coupling_five = coupling(separation, polar_slab, polar_slab, weight, True)
    return field_home(separation, coupling_three, coupling_five, source_slab)

def pair_slab(inputs):
    where_home, polar_home, source_home, where_other, polar_other, source_other = inputs
    separation = where_other[..., None, :] - where_home[..., :, None]
    coupling_three, coupling_five = coupling(separation, polar_home, polar_other, 1.0, False)
    return (field_home(separation, coupling_three, coupling_five, source_other), field_other(separation, coupling_three, coupling_five, source_home))

def operate(vector, positions, polarity, groups, live):
    field_sum = lax.map(self_slab, (positions, polarity, vector, groups))
    for offset in offset_table(True):
        backward = tuple((-int(component) for component in offset))
        forward = tuple((int(component) for component in offset))
        rolled = functools.partial(jnp.roll, shift=backward, axis=(0, 1, 2))
        where_other = rolled(positions) + jnp.asarray(offset, jnp.float32)[:, None] * CELL_EDGE
        home_part, other_part = lax.map(pair_slab, (positions, polarity, vector, where_other, rolled(polarity), rolled(vector)))
        field_sum = field_sum + home_part + jnp.roll(other_part, forward, axis=(0, 1, 2))
    return live[..., None, :] * (vector / polarity[..., None, :] - field_sum)

def reference(positions, polarity, perm_field, groups, occupancy):
    slots = positions.shape[-1]
    live = (jnp.arange(slots, dtype=jnp.int32) < occupancy[..., None]).astype(jnp.float32)
    residual = live[..., None, :] * perm_field
    dipoles = jnp.zeros_like(residual)
    direction = residual
    norm_now = jnp.sum(residual * residual)
    for iteration in range(ITERS):
        applied = operate(direction, positions, polarity, groups, live)
        step_size = norm_now / jnp.sum(direction * applied)
        dipoles = dipoles + step_size * direction
        residual = residual - step_size * applied
        norm_next = jnp.sum(residual * residual)
        direction = residual + norm_next / norm_now * direction
        norm_now = norm_next
    return (dipoles, residual)
```

```python
import functools
import math

import jax
import jax.numpy as jnp
from jax import lax
from jax.experimental import pallas as pl
from jax.experimental.pallas import tpu as pltpu
from jax.sharding import PartitionSpec as P

CL = 128
CELL_EDGE = 11.0
CUTOFF = 9.0
THOLE_A = 0.39
SHIFT = 1.5
AXES = ("gx", "gy", "gz")
MESH = pl.DeviceIdType.MESH
ROWS = 32
BLOCKS = CL // ROWS
HOMES = 2
SELF = 13
UNIT = 1.0 / CUTOFF
LN2 = math.log(2.0)
TOTAL = 3.0 * UNIT**3
F32 = jnp.float32

OFFSETS = sorted(
    [
        (ex, ey, ez)
        for ex in (-1, 0, 1)
        for ey in (-1, 0, 1)
        for ez in (-1, 0, 1)
        if (ex, ey, ez) != (0, 0, 0)
    ],
    key=lambda o: -sum(abs(e) for e in o),
)


def stages(sizes):
    first = [(i, j, 0) for i in range(sizes[0]) for j in range(sizes[1]) if (i, j) != (0, 0)]
    second = [(0, 0, k) for k in range(1, sizes[2])]
    return (first, second)


def kernel(
    sizes,
    pos_ref,
    pol_ref,
    perm_ref,
    grp_ref,
    occ_ref,
    dip_ref,
    res_ref,
    halo,
    halo_v,
    staged,
    home,
    tens,
    acc,
    basis,
    red_a,
    red_b,
    halo_send,
    halo_recv,
    red_send_a,
    red_recv_a,
    red_send_b,
    red_recv_b,
):
    here = tuple(lax.axis_index(a) for a in AXES)
    groups_of = stages(sizes)

    def device(offset):
        return tuple(
            lax.rem(h + (o + n) % n, n) if o else h for h, o, n in zip(here, offset, sizes)
        )

    peers = {tuple((e + n) % n for e, n in zip(o, sizes)) for o in OFFSETS}
    for stage in groups_of:
        peers |= set(stage)
    barrier = pltpu.get_barrier_semaphore()
    for o in sorted(peers):
        pl.semaphore_signal(barrier, inc=1, device_id=device(o), device_id_type=MESH)

    lane = lax.broadcasted_iota(jnp.int32, (1, CL), 1)
    eye = lax.broadcasted_iota(jnp.int32, (CL, CL), 0) == lax.broadcasted_iota(
        jnp.int32, (CL, CL), 1
    )

    live = []
    invpol = []
    for h in range(HOMES):
        alive = (lane < occ_ref[h, 0, 0]).astype(F32)
        live.append(alive)
        pol = pol_ref[h, 0, :, :]
        inv = 1.0 / pol
        invpol.append(inv)
        q = lax.rsqrt(pol)
        mat = jnp.concatenate(
            [
                pos_ref[h, 0, 0] * UNIT,
                q,
                alive * perm_ref[h, 0, 0],
                grp_ref[h, 0, :, :].astype(F32),
            ],
            axis=0,
        )
        halo[1 + h, 4] = mat
        for a in range(3):
            basis[0, h, a] = mat[4 + a : 5 + a]
        cols = jnp.transpose(mat)
        for slot, k in enumerate((0, 1, 2, 3, 7)):
            home[h, slot] = jnp.broadcast_to(cols[:, k : k + 1], (CL, CL))

    pl.semaphore_wait(barrier, len(peers))

    def exchange(buf, k):
        copies = []
        for s, (ex, ey, ez) in enumerate(OFFSETS):
            source, target = 4, (1 - ey) * 3 + (1 - ez)
            if ex == 0:
                src, dst = buf.at[pl.ds(1, 2), source], buf.at[pl.ds(1, 2), target]
            elif ex == 1:
                src, dst = buf.at[2, source], buf.at[0, target]
            else:
                src, dst = buf.at[1, source], buf.at[3, target]
            copies.append(
                pltpu.make_async_remote_copy(
                    src_ref=src,
                    dst_ref=dst,
                    send_sem=halo_send.at[k, s],
                    recv_sem=halo_recv.at[k, s],
                    device_id=device((ex, ey, ez)),
                    device_id_type=MESH,
                )
            )
        for c in copies:
            c.start()
        return copies

    def shifted(x, yz):
        offset = ((x - 1) * CELL_EDGE, (yz // 3 - 1) * CELL_EDGE, (yz % 3 - 1) * CELL_EDGE)
        sub = lax.broadcasted_iota(jnp.int32, (8, CL), 0)
        add = jnp.zeros((8, CL), F32)
        for a in range(3):
            if offset[a]:
                add = jnp.where(sub == a, jnp.float32(offset[a] * UNIT), add)
        staged[x * 9 + yz] = halo[x, yz] + add

    def block_rows(i):
        return pl.ds(pl.multiple_of(i * ROWS, ROWS), ROWS)

    def couple(it, h, i, n, cell, total, own):
        rows = block_rows(i)
        r = [staged[cell, a : a + 1, :] - home[h, a, rows, :] for a in range(3)]
        d2 = r[0] * r[0] + r[1] * r[1] + r[2] * r[2]
        if own:
            diagonal = lax.broadcasted_iota(jnp.int32, (ROWS, CL), 0) + i * ROWS
            diagonal = diagonal == lax.broadcasted_iota(jnp.int32, (ROWS, CL), 1)
            d2 = d2 + diagonal.astype(F32)
        inv = lax.rsqrt(d2)
        inv2 = inv * inv
        taper = jnp.maximum(1.0 - d2, 0.0)
        g = (taper * taper) * (inv2 * inv)
        if own:
            g = jnp.where(staged[cell, 7:8, :] != home[h, 4, rows, :], g, 0.0)
        t = (d2 * d2 * inv) * (home[h, 3, rows, :] * staged[cell, 3:4, :])
        falloff = jnp.exp2(t)
        ge = g * falloff
        c3 = g - ge
        c5 = (c3 + (LN2 * t) * ge) * inv2
        c3 = c3 * (1.0 / 3.0)
        p = [c5 * r[a] for a in range(3)]
        xx = p[0] * r[0] - c3
        yy = p[1] * r[1] - c3
        zz = p[2] * r[2] - c3
        xy = p[0] * r[1]
        xz = p[0] * r[2]
        yz = p[1] * r[2]
        for c, m in enumerate((xx, yy, zz, xy, xz, yz)):
            tens[it, n, c] = m
        v = [staged[cell, 4 + a : 5 + a, :] for a in range(3)]
        return product((xx, yy, zz, xy, xz, yz), v, total)

    def product(m, v, total):
        xx, yy, zz, xy, xz, yz = m
        out = (
            xx * v[0] + xy * v[1] + xz * v[2],
            xy * v[0] + yy * v[1] + yz * v[2],
            xz * v[0] + yz * v[1] + zz * v[2],
        )
        if total is None:
            return out
        return tuple(t + o for t, o in zip(total, out))

    def apply(it, n, v, total):
        return product([tens[it, n, c] for c in range(6)], v, total)

    for h in range(HOMES):
        if h:
            home[h, 0] = home[h, 0] + CELL_EDGE * UNIT * h
        home[h, 3] = home[h, 3] * (-THOLE_A / LN2 / UNIT**3)

    common = [n for n in range(27) if n not in (4, SELF, 22)]

    def inner_first(it, unused):
        h, i = it // BLOCKS, it % BLOCKS
        total = couple(it, h, i, SELF, h * 9 + SELF, None, True)
        total = couple(it, h, i, 22 - 18 * h, (2 - h) * 9 + 4, total, False)
        for a in range(3):
            acc[it, a] = total[a]
        return unused

    def outer_first(it, unused):
        h, i = it // BLOCKS, it % BLOCKS
        total = tuple(acc[it, a] for a in range(3))
        for n in common:
            total = couple(it, h, i, n, h * 9 + n, total, False)
        total = couple(it, h, i, 4 + 18 * h, 27 * h + 4, total, False)
        for a in range(3):
            acc[it, a] = total[a]
        return unused

    def inner_later(k, it, unused):
        h = it // BLOCKS
        total = None
        for n, x in ((SELF, 1 + h), (22 - 18 * h, 2 - h)):
            total = apply(it, n, [halo_v[k, x, 4, a] for a in range(3)], total)
        for a in range(3):
            acc[it, a] = total[a]
        return unused

    def outer_later(k, it, unused):
        h = it // BLOCKS
        total = tuple(acc[it, a] for a in range(3))
        for n in common:
            total = apply(it, n, [halo_v[k, h + n // 9, n % 9, a] for a in range(3)], total)
        total = apply(it, 4 + 18 * h, [halo_v[k, 3 * h, 4, a] for a in range(3)], total)
        for a in range(3):
            acc[it, a] = total[a]
        return unused

    def image(k):
        for h in range(HOMES):
            for a in range(3):
                field = jnp.concatenate([acc[h * BLOCKS + i, a] for i in range(BLOCKS)], axis=0)
                column = jnp.sum(field, axis=1, keepdims=True)
                row = jnp.sum(jnp.where(eye, column, 0.0), axis=0, keepdims=True)
                v = basis[k, h, a]
                nxt = live[h] * (v * invpol[h] - TOTAL * row) - SHIFT * v
                basis[k + 1, h, a] = nxt
                if k < 2:
                    halo_v[k, 1 + h, 4, a] = nxt

    pending = exchange(halo, 0)
    shifted(1, 4)
    shifted(2, 4)
    lax.fori_loop(0, HOMES * BLOCKS, inner_first, 0)
    for c in pending:
        c.wait_recv()
    for x in range(4):
        for yz in range(9):
            if not (yz == 4 and x in (1, 2)):
                shifted(x, yz)
    lax.fori_loop(0, HOMES * BLOCKS, outer_first, 0)
    image(0)
    started = list(pending)
    for k in range(2):
        pending = exchange(halo_v.at[k], 1 + k)
        started += pending
        lax.fori_loop(0, HOMES * BLOCKS, functools.partial(inner_later, k), 0)
        for c in pending:
            c.wait_recv()
        lax.fori_loop(0, HOMES * BLOCKS, functools.partial(outer_later, k), 0)
        image(1 + k)

    row = jnp.zeros((1, CL), F32)
    for m in range(6):
        part = jnp.zeros((1, CL), F32)
        for h in range(HOMES):
            for a in range(3):
                part = part + basis[m // 2, h, a] * basis[(m + 1) // 2, h, a]
        row = jnp.where(lane == m, jnp.sum(part, axis=1, keepdims=True), row)

    for stage, buf, send, recv in (
        (groups_of[0], red_a, red_send_a, red_recv_a),
        (groups_of[1], red_b, red_send_b, red_recv_b),
    ):
        buf[0] = row
        pending = [
            pltpu.make_async_remote_copy(
                src_ref=buf.at[0],
                dst_ref=buf.at[1 + s],
                send_sem=send.at[s],
                recv_sem=recv.at[s],
                device_id=device(o),
                device_id_type=MESH,
            )
            for s, o in enumerate(stage)
        ]
        for c in pending:
            c.start()
        started += pending
        for c in pending:
            c.wait_recv()
        parts = [buf[s] for s in range(1 + len(stage))]
        while len(parts) > 1:
            parts = [
                parts[s] + parts[s + 1] if s + 1 < len(parts) else parts[s]
                for s in range(0, len(parts), 2)
            ]
        row = parts[0]

    moment = [
        jnp.sum(jnp.where(lane == m, row, 0.0), axis=1, keepdims=True) for m in range(6)
    ]

    def dot(left, right):
        total = None
        for i, x in enumerate(left):
            for j, y in enumerate(right):
                term = moment[i + j] * (x * y)
                total = term if total is None else total + term
        return total

    one = jnp.ones((1, 1), F32)
    res, direction, dip = [one], [one], []
    norm = moment[0]
    for iteration in range(3):
        applied = [SHIFT * c for c in direction] + [jnp.zeros((1, 1), F32)]
        applied = [
            c if i == 0 else c + direction[i - 1] for i, c in enumerate(applied)
        ]
        step = norm / dot(direction, applied)
        dip = [
            step * c + (dip[i] if i < len(dip) else 0.0) for i, c in enumerate(direction)
        ]
        res = [
            (res[i] if i < len(res) else 0.0) - step * c for i, c in enumerate(applied)
        ]
        if iteration < 2:
            new = dot(res, res)
            ratio = new / norm
            direction = [
                c + (ratio * direction[i] if i < len(direction) else 0.0)
                for i, c in enumerate(res)
            ]
            norm = new
    for h in range(HOMES):
        for a in range(3):
            v = [basis[k, h, a] for k in range(4)]
            dip_ref[h, 0, 0, a : a + 1, :] = dip[0] * v[0] + dip[1] * v[1] + dip[2] * v[2]
            res_ref[h, 0, 0, a : a + 1, :] = (
                res[0] * v[0] + res[1] * v[1] + res[2] * v[2] + res[3] * v[3]
            )
    for c in started:
        c.wait_send()


def solution(mesh):
    sizes = tuple(mesh.shape[a] for a in AXES)
    first, second = stages(sizes)
    vector = jax.ShapeDtypeStruct((HOMES, 1, 1, 3, CL), F32)
    vmem = pl.BlockSpec(memory_space=pltpu.VMEM)
    call = pl.pallas_call(
        functools.partial(kernel, sizes),
        out_shape=(vector, vector),
        in_specs=[vmem] * 4 + [pl.BlockSpec(memory_space=pltpu.SMEM)],
        out_specs=(vmem, vmem),
        scratch_shapes=[
            pltpu.VMEM((4, 9, 8, CL), F32),
            pltpu.VMEM((2, 4, 9, 3, 1, CL), F32),
            pltpu.VMEM((36, 8, CL), F32),
            pltpu.VMEM((HOMES, 5, CL, CL), F32),
            pltpu.VMEM((HOMES * BLOCKS, 27, 6, ROWS, CL), F32),
            pltpu.VMEM((HOMES * BLOCKS, 3, ROWS, CL), F32),
            pltpu.VMEM((4, HOMES, 3, 1, CL), F32),
            pltpu.VMEM((1 + len(first), 1, CL), F32),
            pltpu.VMEM((1 + len(second), 1, CL), F32),
            pltpu.SemaphoreType.DMA((3, 26)),
            pltpu.SemaphoreType.DMA((3, 26)),
            pltpu.SemaphoreType.DMA((len(first),)),
            pltpu.SemaphoreType.DMA((len(first),)),
            pltpu.SemaphoreType.DMA((len(second),)),
            pltpu.SemaphoreType.DMA((len(second),)),
        ],
        compiler_params=pltpu.CompilerParams(
            collective_id=0, has_side_effects=True, vmem_limit_bytes=48 * 1024 * 1024
        ),
    )
    return jax.shard_map(
        call,
        mesh=mesh,
        in_specs=(
            P("gx", "gy", "gz", None, None),
            P("gx", "gy", "gz", None),
            P("gx", "gy", "gz", None, None),
            P("gx", "gy", "gz", None),
            P("gx", "gy", "gz"),
        ),
        out_specs=(P("gx", "gy", "gz", None, None), P("gx", "gy", "gz", None, None)),
        check_vma=False,
    )
```

```python
import functools
import math

import jax
import jax.numpy as jnp
from jax import lax
from jax.experimental import pallas as pl
from jax.experimental.pallas import tpu as pltpu
from jax.sharding import PartitionSpec as P

CL = 128
CELL_EDGE = 11.0
CUTOFF = 9.0
THOLE_A = 0.39
SHIFT = 1.5
AXES = ("gx", "gy", "gz")
MESH = pl.DeviceIdType.MESH
HOMES = 2
ROWS = 32
BLOCKS = CL // ROWS
TALL = 64
TALLS = CL // TALL
UNIT = 1.0 / CUTOFF
LN2 = math.log(2.0)
TOTAL = 3.0 * UNIT**3
F32 = jnp.float32

FACES = ((-1, 0), (1, 0), (0, -1), (0, 1))
EDGES = ((-1, -1), (-1, 1), (1, -1), (1, 1))

GROUPS = ((2, 10), (12, 16), (28, 8))


def slot_of(dx, dy, dz):
    if dx == 0:
        return 2 + 2 * FACES.index((dy, dz)) if (dy, dz) in FACES else 12 + 2 * EDGES.index((dy, dz))
    side = 0 if dx < 0 else 1
    if (dy, dz) == (0, 0):
        return 10 + side
    if (dy, dz) in FACES:
        return 20 + 4 * side + FACES.index((dy, dz))
    return 28 + 4 * side + EDGES.index((dy, dz))


OFFSETS = sorted(
    [
        (ex, ey, ez)
        for ex in (-1, 0, 1)
        for ey in (-1, 0, 1)
        for ez in (-1, 0, 1)
        if (ex, ey, ez) != (0, 0, 0)
    ],
    key=lambda o: -sum(abs(e) for e in o),
)


def places():
    where = {0: (0, 0, 0), 1: (1, 0, 0)}
    for dx, dy, dz in OFFSETS:
        first = slot_of(dx, dy, dz)
        if dx == 0:
            where[first], where[first + 1] = (0, dy, dz), (1, dy, dz)
        else:
            where[first] = (-1 if dx < 0 else 2, dy, dz)
    return where


PLACES = places()


def stages(sizes):
    first = [(i, j, 0) for i in range(sizes[0]) for j in range(sizes[1]) if (i, j) != (0, 0)]
    second = [(0, 0, k) for k in range(1, sizes[2])]
    return (first, second)


def kernel(
    sizes,
    pos_ref,
    pol_ref,
    perm_ref,
    grp_ref,
    occ_ref,
    dip_ref,
    res_ref,
    inbox,
    inbox_grp,
    inbox_occ,
    halo,
    halo_v,
    staged,
    home,
    tens,
    acc,
    basis,
    red_a,
    red_b,
    in_sem,
    halo_send,
    halo_recv,
    red_send,
    red_recv,
):
    fetches = [
        pltpu.make_async_copy(pos_ref, inbox.at[pl.ds(0, 6)], in_sem.at[0]),
        pltpu.make_async_copy(perm_ref, inbox.at[pl.ds(6, 6)], in_sem.at[1]),
        pltpu.make_async_copy(pol_ref, inbox.at[pl.ds(12, 2)], in_sem.at[2]),
        pltpu.make_async_copy(grp_ref, inbox_grp, in_sem.at[3]),
        pltpu.make_async_copy(occ_ref, inbox_occ, in_sem.at[4]),
    ]
    for c in fetches:
        c.start()

    here = tuple(lax.axis_index(a) for a in AXES)
    near = [
        {
            o: h if o == 0 else lax.rem(h + (o + n), n)
            for o in (-1, 0, 1)
        }
        for h, n in zip(here, sizes)
    ]

    def device(offset):
        return tuple(
            near[d][o] if o in near[d] else lax.rem(here[d] + o, sizes[d])
            for d, o in enumerate(offset)
        )

    groups_of = stages(sizes)

    def wrapped(o):
        return tuple((e + n) % n for e, n in zip(o, sizes))

    peers = list(OFFSETS)
    known = {wrapped(o) for o in OFFSETS}
    for stage in groups_of:
        peers += [o for o in stage if o not in known]
    barrier = pltpu.get_barrier_semaphore()
    for o in peers:
        pl.semaphore_signal(barrier, inc=1, device_id=device(o), device_id_type=MESH)

    lane = lax.broadcasted_iota(jnp.int32, (1, CL), 1)
    eye = lax.broadcasted_iota(jnp.int32, (CL, CL), 0) == lax.broadcasted_iota(
        jnp.int32, (CL, CL), 1
    )

    for c in fetches:
        c.wait()
    live = []
    invpol = []
    for h in range(HOMES):
        alive = (lane < inbox_occ[h]).astype(F32)
        live.append(alive)
        pol = inbox[12 + h]
        invpol.append(1.0 / pol)
        for a in range(3):
            halo[h, a : a + 1, :] = inbox[3 * h + a] * UNIT
            vector = alive * inbox[6 + 3 * h + a]
            halo[h, 4 + a : 5 + a, :] = vector
            basis[0, h, a] = vector
        halo[h, 3:4, :] = lax.rsqrt(pol)
        halo[h, 7:8, :] = inbox_grp[h].astype(F32)

    pl.semaphore_wait(barrier, len(peers))

    def exchange(buf, k):
        for ex, ey, ez in OFFSETS:
            target = slot_of(-ex, -ey, -ez)
            if ex == 0:
                src, dst = buf.at[pl.ds(0, 2)], buf.at[pl.ds(target, 2)]
            else:
                source = 1 if ex == 1 else 0
                src, dst = buf.at[pl.ds(source, 1)], buf.at[pl.ds(target, 1)]
            group = sum(abs(e) for e in (ex, ey, ez)) - 1
            pltpu.make_async_remote_copy(
                src_ref=src,
                dst_ref=dst,
                send_sem=halo_send.at[k],
                recv_sem=halo_recv.at[k, group],
                device_id=device((ex, ey, ez)),
                device_id_type=MESH,
            ).start()

    def arrived(buf, k, group):
        region = buf.at[pl.ds(*GROUPS[group])]
        pltpu.make_async_copy(region, region, halo_recv.at[k, group]).wait()

    def sent(buf, k):
        region = buf.at[pl.ds(2, 34)]
        pltpu.make_async_copy(region, region, halo_send.at[k]).wait()

    def place(slot):
        sub = lax.broadcasted_iota(jnp.int32, (8, CL), 0)
        add = jnp.zeros((8, CL), F32)
        for a in range(3):
            if PLACES[slot][a]:
                add = jnp.where(sub == a, jnp.float32(PLACES[slot][a] * CELL_EDGE * UNIT), add)
        staged[slot] = halo[slot] + add

    def couple(h, i, n, slot, total, own):
        rows = pl.ds(pl.multiple_of(i * ROWS, ROWS), ROWS)
        r = [staged[slot, a : a + 1, :] - home[h, a, rows, :] for a in range(3)]
        d2 = r[0] * r[0] + r[1] * r[1] + r[2] * r[2]
        if own:
            diagonal = lax.broadcasted_iota(jnp.int32, (ROWS, CL), 0) + i * ROWS
            diagonal = diagonal == lax.broadcasted_iota(jnp.int32, (ROWS, CL), 1)
            d2 = d2 + diagonal.astype(F32)
        inv = lax.rsqrt(d2)
        inv2 = inv * inv
        taper = jnp.maximum(1.0 - d2, 0.0)
        g = (taper * taper) * (inv2 * inv)
        if own:
            g = jnp.where(staged[slot, 7:8, :] != home[h, 4, rows, :], g, 0.0)
        t = (d2 * d2 * inv) * (home[h, 3, rows, :] * staged[slot, 3:4, :])
        falloff = jnp.exp2(t)
        ge = g * falloff
        c3 = g - ge
        c5 = (c3 + (LN2 * t) * ge) * inv2
        c3 = c3 * (1.0 / 3.0)
        p = [c5 * r[a] for a in range(3)]
        m = (
            p[0] * r[0] - c3,
            p[1] * r[1] - c3,
            p[2] * r[2] - c3,
            p[0] * r[1],
            p[0] * r[2],
            p[1] * r[2],
        )
        for c in range(6):
            tens[h, n, c, rows, :] = m[c]
        return product(m, [staged[slot, 4 + a : 5 + a, :] for a in range(3)], total)

    def product(m, v, total):
        xx, yy, zz, xy, xz, yz = m
        out = (
            xx * v[0] + xy * v[1] + xz * v[2],
            xy * v[0] + yy * v[1] + yz * v[2],
            xz * v[0] + yz * v[1] + zz * v[2],
        )
        if total is None:
            return out
        return tuple(t + o for t, o in zip(total, out))

    def members(group, h):
        if group == 0:
            return [(n, 2 + n - 2) for n in range(2, 10)] + [(10, 10 + h)]
        if group == 1:
            return [(11 + n, 12 + n) for n in range(8)] + [(19 + n, 20 + 4 * h + n) for n in range(4)]
        return [(23 + n, 28 + 4 * h + n) for n in range(4)]

    def first_own(it, unused):
        h, i = it // BLOCKS, it % BLOCKS
        total = couple(h, i, 0, h, None, True)
        total = couple(h, i, 1, 1 - h, total, False)
        rows = pl.ds(pl.multiple_of(i * ROWS, ROWS), ROWS)
        for a in range(3):
            acc[h, a, rows, :] = total[a]
        return unused

    def first_group(group, it, unused):
        h, i = it // BLOCKS, it % BLOCKS
        rows = pl.ds(pl.multiple_of(i * ROWS, ROWS), ROWS)
        total = tuple(acc[h, a, rows, :] for a in range(3))
        for n, slot in members(group, h):
            total = couple(h, i, n, slot, total, False)
        for a in range(3):
            acc[h, a, rows, :] = total[a]
        return unused

    def apply(k, h, rows, n, slot, total):
        return product(
            [tens[h, n, c, rows, :] for c in range(6)], [halo_v[k, slot, a] for a in range(3)], total
        )

    def later_own(k, it, unused):
        h, i = it // TALLS, it % TALLS
        rows = pl.ds(pl.multiple_of(i * TALL, TALL), TALL)
        total = apply(k, h, rows, 0, h, None)
        total = apply(k, h, rows, 1, 1 - h, total)
        for a in range(3):
            acc[h, a, rows, :] = total[a]
        return unused

    def later_group(k, group, it, unused):
        h, i = it // TALLS, it % TALLS
        rows = pl.ds(pl.multiple_of(i * TALL, TALL), TALL)
        total = tuple(acc[h, a, rows, :] for a in range(3))
        shared = (8, 8, 0)[group]
        rim, slot = ((10, 10 + h), (19, 20 + 4 * h), (23, 28 + 4 * h))[group]
        base = (2, 11, 0)[group]
        if shared:
            total = lax.fori_loop(
                0,
                shared,
                lambda c, t: apply(k, h, rows, base + c, GROUPS[group][0] + c, t),
                total,
            )
        if group == 0:
            total = apply(k, h, rows, rim, slot, total)
        else:
            total = lax.fori_loop(
                0, 4, lambda c, t: apply(k, h, rows, rim + c, slot + c, t), total
            )
        for a in range(3):
            acc[h, a, rows, :] = total[a]
        return unused

    def image(k):
        for h in range(HOMES):
            for a in range(3):
                column = jnp.sum(acc[h, a], axis=1, keepdims=True)
                row = jnp.sum(jnp.where(eye, column, 0.0), axis=0, keepdims=True)
                v = basis[k, h, a]
                nxt = live[h] * (v * invpol[h] - TOTAL * row) - SHIFT * v
                basis[k + 1, h, a] = nxt
                if k < 2:
                    halo_v[k, h, a] = nxt

    exchange(halo, 0)
    for h in range(HOMES):
        place(h)
        cols = jnp.transpose(staged[h])
        for entry, c in enumerate((0, 1, 2, 3, 7)):
            col = cols[:, c : c + 1]
            if c == 3:
                col = col * (-THOLE_A / LN2 / UNIT**3)
            home[h, entry] = jnp.broadcast_to(col, (CL, CL))
    lax.fori_loop(0, HOMES * BLOCKS, first_own, 0)
    for group in range(3):
        arrived(halo, 0, group)
        for slot in range(GROUPS[group][0], sum(GROUPS[group])):
            place(slot)
        lax.fori_loop(0, HOMES * BLOCKS, functools.partial(first_group, group), 0)
    image(0)
    for k in range(2):
        exchange(halo_v.at[k], 1 + k)
        lax.fori_loop(0, HOMES * TALLS, functools.partial(later_own, k), 0)
        for group in range(3):
            arrived(halo_v.at[k], 1 + k, group)
            lax.fori_loop(0, HOMES * TALLS, functools.partial(later_group, k, group), 0)
        image(1 + k)

    row = jnp.zeros((1, CL), F32)
    for m in range(6):
        part = jnp.zeros((1, CL), F32)
        for h in range(HOMES):
            for a in range(3):
                part = part + basis[m // 2, h, a] * basis[(m + 1) // 2, h, a]
        row = jnp.where(lane == m, jnp.sum(part, axis=1, keepdims=True), row)

    for s, (stage, buf) in enumerate(zip(groups_of, (red_a, red_b))):
        buf[0] = row
        for i, o in enumerate(stage):
            pltpu.make_async_remote_copy(
                src_ref=buf.at[0],
                dst_ref=buf.at[1 + i],
                send_sem=red_send.at[s],
                recv_sem=red_recv.at[s],
                device_id=device(o),
                device_id_type=MESH,
            ).start()
        region = buf.at[pl.ds(1, len(stage))]
        pltpu.make_async_copy(region, region, red_recv.at[s]).wait()
        parts = [buf[i] for i in range(1 + len(stage))]
        while len(parts) > 1:
            parts = [
                parts[i] + parts[i + 1] if i + 1 < len(parts) else parts[i]
                for i in range(0, len(parts), 2)
            ]
        row = parts[0]

    moment = [
        jnp.sum(jnp.where(lane == m, row, 0.0), axis=1, keepdims=True) for m in range(6)
    ]

    def dot(left, right):
        total = None
        for i, x in enumerate(left):
            for j, y in enumerate(right):
                term = moment[i + j] * (x * y)
                total = term if total is None else total + term
        return total

    one = jnp.ones((1, 1), F32)
    res, direction, dip = [one], [one], []
    norm = moment[0]
    for iteration in range(3):
        applied = [SHIFT * c for c in direction] + [jnp.zeros((1, 1), F32)]
        applied = [
            c if i == 0 else c + direction[i - 1] for i, c in enumerate(applied)
        ]
        step = norm / dot(direction, applied)
        dip = [
            step * c + (dip[i] if i < len(dip) else 0.0) for i, c in enumerate(direction)
        ]
        res = [
            (res[i] if i < len(res) else 0.0) - step * c for i, c in enumerate(applied)
        ]
        if iteration < 2:
            new = dot(res, res)
            ratio = new / norm
            direction = [
                c + (ratio * direction[i] if i < len(direction) else 0.0)
                for i, c in enumerate(res)
            ]
            norm = new
    for h in range(HOMES):
        for a in range(3):
            v = [basis[k, h, a] for k in range(4)]
            dip_ref[3 * h + a] = dip[0] * v[0] + dip[1] * v[1] + dip[2] * v[2]
            res_ref[3 * h + a] = res[0] * v[0] + res[1] * v[1] + res[2] * v[2] + res[3] * v[3]
    sent(halo, 0)
    for k in range(2):
        sent(halo_v.at[k], 1 + k)
    for s, (stage, buf) in enumerate(zip(groups_of, (red_a, red_b))):
        region = buf.at[pl.ds(1, len(stage))]
        pltpu.make_async_copy(region, region, red_send.at[s]).wait()


def solution(mesh):
    sizes = tuple(mesh.shape[a] for a in AXES)
    first, second = stages(sizes)
    vector = jax.ShapeDtypeStruct((HOMES * 3, 1, CL), F32)
    vmem = pl.BlockSpec(memory_space=pltpu.VMEM)
    call = pl.pallas_call(
        functools.partial(kernel, sizes),
        out_shape=(vector, vector),
        in_specs=[pl.BlockSpec(memory_space=pl.ANY)] * 5,
        out_specs=(vmem, vmem),
        scratch_shapes=[
            pltpu.VMEM((14, 1, CL), F32),
            pltpu.VMEM((HOMES, 1, CL), jnp.int32),
            pltpu.SMEM((HOMES,), jnp.int32),
            pltpu.VMEM((36, 8, CL), F32),
            pltpu.VMEM((2, 36, 3, 1, CL), F32),
            pltpu.VMEM((36, 8, CL), F32),
            pltpu.VMEM((HOMES, 5, CL, CL), F32),
            pltpu.VMEM((HOMES, 27, 6, CL, CL), F32),
            pltpu.VMEM((HOMES, 3, CL, CL), F32),
            pltpu.VMEM((4, HOMES, 3, 1, CL), F32),
            pltpu.VMEM((1 + len(first), 1, CL), F32),
            pltpu.VMEM((1 + len(second), 1, CL), F32),
            pltpu.SemaphoreType.DMA((5,)),
            pltpu.SemaphoreType.DMA((3,)),
            pltpu.SemaphoreType.DMA((3, 3)),
            pltpu.SemaphoreType.DMA((2,)),
            pltpu.SemaphoreType.DMA((2,)),
        ],
        compiler_params=pltpu.CompilerParams(
            collective_id=0, has_side_effects=True, vmem_limit_bytes=62 * 1024 * 1024
        ),
    )

    def shards(positions, polarity, perm_field, groups, occupancy):
        dipoles, residual = call(
            positions.reshape(HOMES * 3, 1, CL),
            polarity.reshape(HOMES, 1, CL),
            perm_field.reshape(HOMES * 3, 1, CL),
            groups.reshape(HOMES, 1, CL),
            occupancy.reshape(HOMES),
        )
        return dipoles.reshape(positions.shape), residual.reshape(positions.shape)

    return jax.shard_map(
        shards,
        mesh=mesh,
        in_specs=(
            P("gx", "gy", "gz", None, None),
            P("gx", "gy", "gz", None),
            P("gx", "gy", "gz", None, None),
            P("gx", "gy", "gz", None),
            P("gx", "gy", "gz"),
        ),
        out_specs=(P("gx", "gy", "gz", None, None), P("gx", "gy", "gz", None, None)),
        check_vma=False,
    )
```

```python
import functools
import math

import jax
import jax.numpy as jnp
from jax import lax
from jax.experimental import pallas as pl
from jax.experimental.pallas import tpu as pltpu
from jax.sharding import PartitionSpec as P

CL = 128
CELL_EDGE = 11.0
CUTOFF = 9.0
THOLE_A = 0.39
SHIFT = 1.5
AXES = ("gx", "gy", "gz")
MESH = pl.DeviceIdType.MESH
HOMES = 2
ROWS = 32
BLOCKS = CL // ROWS
TALL = 64
TALLS = CL // TALL
CHUNK = 4
UNIT = 1.0 / CUTOFF
LN2 = math.log(2.0)
TOTAL = 3.0 * UNIT**3
F32 = jnp.float32

FACES = ((-1, 0), (1, 0), (0, -1), (0, 1))
EDGES = ((-1, -1), (-1, 1), (1, -1), (1, 1))

GROUPS = ((2, 10), (12, 16), (28, 8))


def slot_of(dx, dy, dz):
    if dx == 0:
        return 2 + 2 * FACES.index((dy, dz)) if (dy, dz) in FACES else 12 + 2 * EDGES.index((dy, dz))
    side = 0 if dx < 0 else 1
    if (dy, dz) == (0, 0):
        return 10 + side
    if (dy, dz) in FACES:
        return 20 + 4 * side + FACES.index((dy, dz))
    return 28 + 4 * side + EDGES.index((dy, dz))


OFFSETS = sorted(
    [
        (ex, ey, ez)
        for ex in (-1, 0, 1)
        for ey in (-1, 0, 1)
        for ez in (-1, 0, 1)
        if (ex, ey, ez) != (0, 0, 0)
    ],
    key=lambda o: -sum(abs(e) for e in o),
)


def places():
    where = {0: (0, 0, 0), 1: (1, 0, 0)}
    for dx, dy, dz in OFFSETS:
        first = slot_of(dx, dy, dz)
        if dx == 0:
            where[first], where[first + 1] = (0, dy, dz), (1, dy, dz)
        else:
            where[first] = (-1 if dx < 0 else 2, dy, dz)
    return where


PLACES = places()


def stages(sizes):
    first = [(i, j, 0) for i in range(sizes[0]) for j in range(sizes[1]) if (i, j) != (0, 0)]
    second = [(0, 0, k) for k in range(1, sizes[2])]
    return (first, second)


def kernel(
    sizes,
    pos_ref,
    pol_ref,
    perm_ref,
    grp_ref,
    occ_ref,
    out_ref,
    inbox,
    inbox_grp,
    inbox_occ,
    halo,
    halo_v,
    staged,
    home,
    tens,
    acc,
    basis,
    red_a,
    red_b,
    in_sem,
    halo_send,
    halo_recv,
    red_send,
    red_recv,
    greeted,
):
    fetches = [
        pltpu.make_async_copy(pos_ref, inbox.at[pl.ds(0, 6)], in_sem.at[0]),
        pltpu.make_async_copy(perm_ref, inbox.at[pl.ds(6, 6)], in_sem.at[1]),
        pltpu.make_async_copy(pol_ref, inbox.at[pl.ds(12, 2)], in_sem.at[2]),
        pltpu.make_async_copy(grp_ref, inbox_grp, in_sem.at[3]),
        pltpu.make_async_copy(occ_ref, inbox_occ, in_sem.at[4]),
    ]
    for c in fetches:
        c.start()

    here = tuple(lax.axis_index(a) for a in AXES)
    near = [
        {
            o: h if o == 0 else lax.rem(h + (o + n), n)
            for o in (-1, 0, 1)
        }
        for h, n in zip(here, sizes)
    ]

    def device(offset):
        return tuple(
            near[d][o] if o in near[d] else lax.rem(here[d] + o, sizes[d])
            for d, o in enumerate(offset)
        )

    groups_of = stages(sizes)
    barrier = pltpu.get_barrier_semaphore()
    for o in reversed(OFFSETS):
        pl.semaphore_signal(barrier, inc=1, device_id=device(o), device_id_type=MESH)

    def greet(step, reach):
        for o in (reach, sizes[2] - reach):
            pl.semaphore_signal(
                greeted.at[step], inc=1, device_id=device((0, 0, o)), device_id_type=MESH
            )

    lane = lax.broadcasted_iota(jnp.int32, (1, CL), 1)
    eye = lax.broadcasted_iota(jnp.int32, (CL, CL), 0) == lax.broadcasted_iota(
        jnp.int32, (CL, CL), 1
    )

    for c in fetches:
        c.wait()
    live = []
    invpol = []
    for h in range(HOMES):
        alive = (lane < inbox_occ[h]).astype(F32)
        live.append(alive)
        pol = inbox[12 + h]
        invpol.append(1.0 / pol)
        for a in range(3):
            halo[h, a : a + 1, :] = inbox[3 * h + a] * UNIT
            vector = alive * inbox[6 + 3 * h + a]
            halo[h, 4 + a : 5 + a, :] = vector
            basis[0, h, a] = vector
        halo[h, 3:4, :] = lax.rsqrt(pol)
        halo[h, 7:8, :] = inbox_grp[h].astype(F32)

    pl.semaphore_wait(barrier, len(OFFSETS))

    def exchange(buf, k):
        for ex, ey, ez in OFFSETS:
            target = slot_of(-ex, -ey, -ez)
            if ex == 0:
                src, dst = buf.at[pl.ds(0, 2)], buf.at[pl.ds(target, 2)]
            else:
                source = 1 if ex == 1 else 0
                src, dst = buf.at[pl.ds(source, 1)], buf.at[pl.ds(target, 1)]
            group = sum(abs(e) for e in (ex, ey, ez)) - 1
            pltpu.make_async_remote_copy(
                src_ref=src,
                dst_ref=dst,
                send_sem=halo_send.at[k],
                recv_sem=halo_recv.at[k, group],
                device_id=device((ex, ey, ez)),
                device_id_type=MESH,
            ).start()

    def arrived(buf, k, group):
        region = buf.at[pl.ds(*GROUPS[group])]
        pltpu.make_async_copy(region, region, halo_recv.at[k, group]).wait()

    def sent(buf, k):
        region = buf.at[pl.ds(2, 34)]
        pltpu.make_async_copy(region, region, halo_send.at[k]).wait()

    def place(slot):
        sub = lax.broadcasted_iota(jnp.int32, (8, CL), 0)
        add = jnp.zeros((8, CL), F32)
        for a in range(3):
            if PLACES[slot][a]:
                add = jnp.where(sub == a, jnp.float32(PLACES[slot][a] * CELL_EDGE * UNIT), add)
        staged[slot] = halo[slot] + add

    def couple(h, i, n, slot, total, own):
        rows = pl.ds(pl.multiple_of(i * ROWS, ROWS), ROWS)
        r = [staged[slot, a : a + 1, :] - home[h, a, rows, :] for a in range(3)]
        d2 = r[0] * r[0] + r[1] * r[1] + r[2] * r[2]
        if own:
            diagonal = lax.broadcasted_iota(jnp.int32, (ROWS, CL), 0) + i * ROWS
            diagonal = diagonal == lax.broadcasted_iota(jnp.int32, (ROWS, CL), 1)
            d2 = d2 + diagonal.astype(F32)
        inv = lax.rsqrt(d2)
        inv2 = inv * inv
        taper = jnp.maximum(1.0 - d2, 0.0)
        g = (taper * taper) * (inv2 * inv)
        if own:
            g = jnp.where(staged[slot, 7:8, :] != home[h, 4, rows, :], g, 0.0)
        t = (d2 * d2 * inv) * (home[h, 3, rows, :] * staged[slot, 3:4, :])
        falloff = jnp.exp2(t)
        ge = g * falloff
        c3 = g - ge
        c5 = (c3 + (LN2 * t) * ge) * inv2
        c3 = c3 * (1.0 / 3.0)
        p = [c5 * r[a] for a in range(3)]
        m = (
            p[0] * r[0] - c3,
            p[1] * r[1] - c3,
            p[2] * r[2] - c3,
            p[0] * r[1],
            p[0] * r[2],
            p[1] * r[2],
        )
        for c in range(6):
            tens[h, n, c, rows, :] = m[c]
        return product(m, [staged[slot, 4 + a : 5 + a, :] for a in range(3)], total)

    def product(m, v, total):
        xx, yy, zz, xy, xz, yz = m
        out = []
        for a, line in enumerate(((xx, xy, xz), (xy, yy, yz), (xz, yz, zz))):
            total_a = line[0] * v[0] if total is None else total[a] + line[0] * v[0]
            out.append((total_a + line[1] * v[1]) + line[2] * v[2])
        return tuple(out)

    def members(group, h):
        if group == 0:
            return [(n, 2 + n - 2) for n in range(2, 10)] + [(10, 10 + h)]
        if group == 1:
            return [(11 + n, 12 + n) for n in range(8)] + [(19 + n, 20 + 4 * h + n) for n in range(4)]
        return [(23 + n, 28 + 4 * h + n) for n in range(4)]

    def first_own(it, unused):
        h, i = it // BLOCKS, it % BLOCKS
        total = couple(h, i, 0, h, None, True)
        total = couple(h, i, 1, 1 - h, total, False)
        rows = pl.ds(pl.multiple_of(i * ROWS, ROWS), ROWS)
        for a in range(3):
            acc[h, a, rows, :] = total[a]
        return unused

    def first_group(group, it, unused):
        h, i = it // BLOCKS, it % BLOCKS
        rows = pl.ds(pl.multiple_of(i * ROWS, ROWS), ROWS)
        total = tuple(acc[h, a, rows, :] for a in range(3))
        for n, slot in members(group, h):
            total = couple(h, i, n, slot, total, False)
        for a in range(3):
            acc[h, a, rows, :] = total[a]
        return unused

    def apply(k, h, rows, n, slot, total):
        return product(
            [tens[h, n, c, rows, :] for c in range(6)], [halo_v[k, slot, a] for a in range(3)], total
        )

    def later_own(k, it, unused):
        h, i = it // TALLS, it % TALLS
        rows = pl.ds(pl.multiple_of(i * TALL, TALL), TALL)
        total = apply(k, h, rows, 0, h, None)
        total = apply(k, h, rows, 1, 1 - h, total)
        for a in range(3):
            acc[h, a, rows, :] = total[a]
        return unused

    def later_group(k, group, it, unused):
        h, i = it // TALLS, it % TALLS
        rows = pl.ds(pl.multiple_of(i * TALL, TALL), TALL)
        total = tuple(acc[h, a, rows, :] for a in range(3))
        shared = (8, 8, 0)[group]
        rim, slot = ((10, 10 + h), (19, 20 + 4 * h), (23, 28 + 4 * h))[group]
        base = (2, 11, 0)[group]

        def step(first, at, count, total):
            for c in range(count):
                total = apply(k, h, rows, first + c, at + c, total)
            return total

        if shared:
            total = lax.fori_loop(
                0,
                shared // CHUNK,
                lambda c, t: step(base + CHUNK * c, GROUPS[group][0] + CHUNK * c, CHUNK, t),
                total,
            )
        total = step(rim, slot, 1 if group == 0 else 4, total)
        for a in range(3):
            acc[h, a, rows, :] = total[a]
        return unused

    def image(k):
        for h in range(HOMES):
            for a in range(3):
                column = jnp.sum(acc[h, a], axis=1, keepdims=True)
                row = jnp.sum(jnp.where(eye, column, 0.0), axis=0, keepdims=True)
                v = basis[k, h, a]
                nxt = live[h] * (v * invpol[h] - TOTAL * row) - SHIFT * v
                basis[k + 1, h, a] = nxt
                if k < 2:
                    halo_v[k, h, a] = nxt

    exchange(halo, 0)
    for h in range(HOMES):
        place(h)
        cols = jnp.transpose(staged[h])
        for entry, c in enumerate((0, 1, 2, 3, 7)):
            col = cols[:, c : c + 1]
            if c == 3:
                col = col * (-THOLE_A / LN2 / UNIT**3)
            home[h, entry] = jnp.broadcast_to(col, (CL, CL))
    lax.fori_loop(0, HOMES * BLOCKS, first_own, 0)
    for group in range(3):
        arrived(halo, 0, group)
        for slot in range(GROUPS[group][0], sum(GROUPS[group])):
            place(slot)
        lax.fori_loop(0, HOMES * BLOCKS, functools.partial(first_group, group), 0)
    greet(0, 2)
    image(0)
    for k in range(2):
        exchange(halo_v.at[k], 1 + k)
        lax.fori_loop(0, HOMES * TALLS, functools.partial(later_own, k), 0)
        for group in range(3):
            arrived(halo_v.at[k], 1 + k, group)
            lax.fori_loop(0, HOMES * TALLS, functools.partial(later_group, k, group), 0)
        pl.semaphore_wait(greeted.at[k], 2)
        if k == 0:
            greet(1, 4)
        image(1 + k)

    row = jnp.zeros((1, CL), F32)
    for m in range(6):
        part = jnp.zeros((1, CL), F32)
        for h in range(HOMES):
            for a in range(3):
                part = part + basis[m // 2, h, a] * basis[(m + 1) // 2, h, a]
        row = jnp.where(lane == m, jnp.sum(part, axis=1, keepdims=True), row)

    for s, (stage, buf) in enumerate(zip(groups_of, (red_a, red_b))):
        buf[0] = row
        for i, o in enumerate(stage):
            pltpu.make_async_remote_copy(
                src_ref=buf.at[0],
                dst_ref=buf.at[1 + i],
                send_sem=red_send.at[s],
                recv_sem=red_recv.at[s],
                device_id=device(o),
                device_id_type=MESH,
            ).start()
        region = buf.at[pl.ds(1, len(stage))]
        pltpu.make_async_copy(region, region, red_recv.at[s]).wait()
        parts = [buf[i] for i in range(1 + len(stage))]
        while len(parts) > 1:
            parts = [
                parts[i] + parts[i + 1] if i + 1 < len(parts) else parts[i]
                for i in range(0, len(parts), 2)
            ]
        row = parts[0]

    moment = [
        jnp.sum(jnp.where(lane == m, row, 0.0), axis=1, keepdims=True) for m in range(6)
    ]

    def dot(left, right):
        total = None
        for i, x in enumerate(left):
            for j, y in enumerate(right):
                term = moment[i + j] * (x * y)
                total = term if total is None else total + term
        return total

    one = jnp.ones((1, 1), F32)
    res, direction, dip = [one], [one], []
    norm = moment[0]
    for iteration in range(3):
        applied = [SHIFT * c for c in direction] + [jnp.zeros((1, 1), F32)]
        applied = [
            c if i == 0 else c + direction[i - 1] for i, c in enumerate(applied)
        ]
        step = norm / dot(direction, applied)
        dip = [
            step * c + (dip[i] if i < len(dip) else 0.0) for i, c in enumerate(direction)
        ]
        res = [
            (res[i] if i < len(res) else 0.0) - step * c for i, c in enumerate(applied)
        ]
        if iteration < 2:
            new = dot(res, res)
            ratio = new / norm
            direction = [
                c + (ratio * direction[i] if i < len(direction) else 0.0)
                for i, c in enumerate(res)
            ]
            norm = new
    for h in range(HOMES):
        for a in range(3):
            v = [basis[k, h, a] for k in range(4)]
            out_ref[3 * h + a] = dip[0] * v[0] + dip[1] * v[1] + dip[2] * v[2]
            out_ref[6 + 3 * h + a] = res[0] * v[0] + res[1] * v[1] + res[2] * v[2] + res[3] * v[3]
    sent(halo, 0)
    for k in range(2):
        sent(halo_v.at[k], 1 + k)
    for s, (stage, buf) in enumerate(zip(groups_of, (red_a, red_b))):
        region = buf.at[pl.ds(1, len(stage))]
        pltpu.make_async_copy(region, region, red_send.at[s]).wait()


def solution(mesh):
    sizes = tuple(mesh.shape[a] for a in AXES)
    first, second = stages(sizes)
    vector = jax.ShapeDtypeStruct((2 * HOMES * 3, 1, CL), F32)
    vmem = pl.BlockSpec(memory_space=pltpu.VMEM)
    call = pl.pallas_call(
        functools.partial(kernel, sizes),
        out_shape=vector,
        in_specs=[pl.BlockSpec(memory_space=pl.ANY)] * 5,
        out_specs=vmem,
        scratch_shapes=[
            pltpu.VMEM((14, 1, CL), F32),
            pltpu.VMEM((HOMES, 1, CL), jnp.int32),
            pltpu.SMEM((HOMES,), jnp.int32),
            pltpu.VMEM((36, 8, CL), F32),
            pltpu.VMEM((2, 36, 3, 1, CL), F32),
            pltpu.VMEM((36, 8, CL), F32),
            pltpu.VMEM((HOMES, 5, CL, CL), F32),
            pltpu.VMEM((HOMES, 27, 6, CL, CL), F32),
            pltpu.VMEM((HOMES, 3, CL, CL), F32),
            pltpu.VMEM((4, HOMES, 3, 1, CL), F32),
            pltpu.VMEM((1 + len(first), 1, CL), F32),
            pltpu.VMEM((1 + len(second), 1, CL), F32),
            pltpu.SemaphoreType.DMA((5,)),
            pltpu.SemaphoreType.DMA((3,)),
            pltpu.SemaphoreType.DMA((3, 3)),
            pltpu.SemaphoreType.DMA((2,)),
            pltpu.SemaphoreType.DMA((2,)),
            pltpu.SemaphoreType.REGULAR((2,)),
        ],
        compiler_params=pltpu.CompilerParams(
            collective_id=0, has_side_effects=True, vmem_limit_bytes=62 * 1024 * 1024
        ),
    )

    def shards(positions, polarity, perm_field, groups, occupancy):
        both = call(
            positions.reshape(HOMES * 3, 1, CL),
            polarity.reshape(HOMES, 1, CL),
            perm_field.reshape(HOMES * 3, 1, CL),
            groups.reshape(HOMES, 1, CL),
            occupancy.reshape(HOMES),
        )
        return both[:6].reshape(positions.shape), both[6:].reshape(positions.shape)

    return jax.shard_map(
        shards,
        mesh=mesh,
        in_specs=(
            P("gx", "gy", "gz", None, None),
            P("gx", "gy", "gz", None),
            P("gx", "gy", "gz", None, None),
            P("gx", "gy", "gz", None),
            P("gx", "gy", "gz"),
        ),
        out_specs=(P("gx", "gy", "gz", None, None), P("gx", "gy", "gz", None, None)),
        check_vma=False,
    )
```

```python
import functools
import math

import jax
import jax.numpy as jnp
from jax import lax
from jax.experimental import pallas as pl
from jax.experimental.pallas import tpu as pltpu
from jax.sharding import PartitionSpec as P

CL = 128
CELL_EDGE = 11.0
CUTOFF = 9.0
THOLE_A = 0.39
SHIFT = 1.5
AXES = ("gx", "gy", "gz")
MESH = pl.DeviceIdType.MESH
HOMES = 2
ROWS = 32
BLOCKS = CL // ROWS
TALL = 64
TALLS = CL // TALL
CHUNK = 4
UNIT = 1.0 / CUTOFF
LN2 = math.log(2.0)
TINY = 1e-36
TOTAL = 3.0 * UNIT**3
F32 = jnp.float32

FACES = ((-1, 0), (1, 0), (0, -1), (0, 1))
EDGES = ((-1, -1), (-1, 1), (1, -1), (1, 1))

GROUPS = ((2, 10), (12, 16), (28, 8))


def slot_of(dx, dy, dz):
    if dx == 0:
        return 2 + 2 * FACES.index((dy, dz)) if (dy, dz) in FACES else 12 + 2 * EDGES.index((dy, dz))
    side = 0 if dx < 0 else 1
    if (dy, dz) == (0, 0):
        return 10 + side
    if (dy, dz) in FACES:
        return 20 + 4 * side + FACES.index((dy, dz))
    return 28 + 4 * side + EDGES.index((dy, dz))


OFFSETS = sorted(
    [
        (ex, ey, ez)
        for ex in (-1, 0, 1)
        for ey in (-1, 0, 1)
        for ez in (-1, 0, 1)
        if (ex, ey, ez) != (0, 0, 0)
    ],
    key=lambda o: sum(abs(e) for e in o),
)


def places():
    where = {0: (0, 0, 0), 1: (1, 0, 0)}
    for dx, dy, dz in OFFSETS:
        first = slot_of(dx, dy, dz)
        if dx == 0:
            where[first], where[first + 1] = (0, dy, dz), (1, dy, dz)
        else:
            where[first] = (-1 if dx < 0 else 2, dy, dz)
    return where


PLACES = places()


def stages(sizes):
    def way(o):
        return -sum(min(e, n - e) for e, n in zip(o, sizes))

    first = [(i, j, 0) for i in range(sizes[0]) for j in range(sizes[1]) if (i, j) != (0, 0)]
    second = [(0, 0, k) for k in range(1, sizes[2])]
    return (sorted(first, key=way), sorted(second, key=way))


def kernel(
    sizes,
    pos_ref,
    pol_ref,
    perm_ref,
    grp_ref,
    occ_ref,
    out_ref,
    inbox,
    inbox_grp,
    inbox_occ,
    halo,
    halo_v,
    staged,
    home,
    tens,
    acc,
    basis,
    red_a,
    red_b,
    in_sem,
    halo_send,
    halo_recv,
    red_send,
    red_recv,
    greeted,
):
    fetches = [
        pltpu.make_async_copy(pos_ref, inbox.at[pl.ds(0, 6)], in_sem.at[0]),
        pltpu.make_async_copy(perm_ref, inbox.at[pl.ds(6, 6)], in_sem.at[1]),
        pltpu.make_async_copy(pol_ref, inbox.at[pl.ds(12, 2)], in_sem.at[2]),
        pltpu.make_async_copy(grp_ref, inbox_grp, in_sem.at[3]),
        pltpu.make_async_copy(occ_ref, inbox_occ, in_sem.at[4]),
    ]
    for c in fetches:
        c.start()

    here = tuple(lax.axis_index(a) for a in AXES)
    near = [
        {
            o: h if o == 0 else lax.rem(h + (o + n), n)
            for o in (-1, 0, 1)
        }
        for h, n in zip(here, sizes)
    ]

    def device(offset):
        return tuple(
            near[d][o] if o in near[d] else lax.rem(here[d] + o, sizes[d])
            for d, o in enumerate(offset)
        )

    groups_of = stages(sizes)
    barrier = pltpu.get_barrier_semaphore()
    for o in OFFSETS:
        pl.semaphore_signal(barrier, inc=1, device_id=device(o), device_id_type=MESH)

    def greet(step, reach):
        for o in (reach, sizes[2] - reach):
            pl.semaphore_signal(
                greeted.at[step], inc=1, device_id=device((0, 0, o)), device_id_type=MESH
            )

    lane = lax.broadcasted_iota(jnp.int32, (1, CL), 1)
    eye = lax.broadcasted_iota(jnp.int32, (CL, CL), 0) == lax.broadcasted_iota(
        jnp.int32, (CL, CL), 1
    )

    for c in fetches:
        c.wait()
    live = []
    invpol = []
    for h in range(HOMES):
        alive = (lane < inbox_occ[h]).astype(F32)
        live.append(alive)
        pol = inbox[12 + h]
        invpol.append(1.0 / pol)
        for a in range(3):
            halo[h, a : a + 1, :] = inbox[3 * h + a] * UNIT
            vector = alive * inbox[6 + 3 * h + a]
            halo[h, 4 + a : 5 + a, :] = vector
            basis[0, h, a] = vector
        halo[h, 3:4, :] = lax.rsqrt(pol)
        halo[h, 7:8, :] = inbox_grp[h].astype(F32)

    pl.semaphore_wait(barrier, len(OFFSETS))

    def exchange(buf, k):
        for ex, ey, ez in OFFSETS:
            target = slot_of(-ex, -ey, -ez)
            if ex == 0:
                src, dst = buf.at[pl.ds(0, 2)], buf.at[pl.ds(target, 2)]
            else:
                source = 1 if ex == 1 else 0
                src, dst = buf.at[pl.ds(source, 1)], buf.at[pl.ds(target, 1)]
            group = sum(abs(e) for e in (ex, ey, ez)) - 1
            pltpu.make_async_remote_copy(
                src_ref=src,
                dst_ref=dst,
                send_sem=halo_send.at[k],
                recv_sem=halo_recv.at[k, group],
                device_id=device((ex, ey, ez)),
                device_id_type=MESH,
            ).start()

    def arrived(buf, k, group):
        region = buf.at[pl.ds(*GROUPS[group])]
        pltpu.make_async_copy(region, region, halo_recv.at[k, group]).wait()

    def sent(buf, k):
        region = buf.at[pl.ds(2, 34)]
        pltpu.make_async_copy(region, region, halo_send.at[k]).wait()

    def place(slot):
        sub = lax.broadcasted_iota(jnp.int32, (8, CL), 0)
        add = jnp.zeros((8, CL), F32)
        for a in range(3):
            if PLACES[slot][a]:
                add = jnp.where(sub == a, jnp.float32(PLACES[slot][a] * CELL_EDGE * UNIT), add)
        staged[slot] = halo[slot] + add

    def couple_tile(h, first, n, slot, total, own):
        rows = pl.ds(first, 8)
        r = [staged[slot, a : a + 1, :] - home[h, a, rows, :] for a in range(3)]
        d2 = r[0] * r[0] + r[1] * r[1] + r[2] * r[2]
        if own:
            diagonal = lax.broadcasted_iota(jnp.int32, (8, CL), 0) + first
            diagonal = diagonal == lax.broadcasted_iota(jnp.int32, (8, CL), 1)
            d2 = d2 + diagonal.astype(F32)
        inv = lax.rsqrt(d2)
        taper = jnp.maximum(1.0 - d2, 0.0)
        scaled = taper * inv
        g = (scaled * scaled) * inv
        if own:
            g = jnp.where(staged[slot, 7:8, :] != home[h, 4, rows, :], g, 0.0)
        t = (d2 * d2 * inv) * (home[h, 3, rows, :] * staged[slot, 3:4, :])
        ge = g * jnp.exp2(t)
        c3 = g - ge
        z = jnp.maximum(c3 + (LN2 * t) * ge, TINY)
        f = (z * lax.rsqrt(z)) * inv
        m = (f * r[0], f * r[1], f * r[2], c3 * (1.0 / 3.0))
        for c in range(4):
            tens[h, n, c, rows, :] = m[c]
        return product(m, [staged[slot, 4 + a : 5 + a, :] for a in range(3)], total)

    def couple(h, i, n, slot, total, own):
        out = []
        for tile in range(ROWS // 8):
            first = pl.multiple_of(i * ROWS + 8 * tile, 8)
            part = None if total is None else total[3 * tile : 3 * tile + 3]
            out += couple_tile(h, first, n, slot, part, own)
        return tuple(out)

    def product(m, v, total):
        s = m[0] * v[0] + m[1] * v[1] + m[2] * v[2]
        out = [m[a] * s - m[3] * v[a] for a in range(3)]
        return tuple(out if total is None else (t + o for t, o in zip(total, out)))

    def members(group, h):
        if group == 0:
            return [(n, 2 + n - 2) for n in range(2, 10)] + [(10, 10 + h)]
        if group == 1:
            return [(11 + n, 12 + n) for n in range(8)] + [(19 + n, 20 + 4 * h + n) for n in range(4)]
        return [(23 + n, 28 + 4 * h + n) for n in range(4)]

    def first_own(it, unused):
        h, i = it // BLOCKS, it % BLOCKS
        total = couple(h, i, 0, h, None, True)
        total = couple(h, i, 1, 1 - h, total, False)
        closed(h, i * ROWS, total)
        return unused

    def first_group(group, it, unused):
        h, i = it // BLOCKS, it % BLOCKS
        total = opened(h, i * ROWS, ROWS)
        for n, slot in members(group, h):
            total = couple(h, i, n, slot, total, False)
        closed(h, i * ROWS, total)
        return unused

    def apply(k, h, first, n, slot, total):
        v = [halo_v[k, slot, a] for a in range(3)]
        out = []
        for tile in range(TALL // 8):
            rows = pl.ds(pl.multiple_of(first + 8 * tile, 8), 8)
            part = None if total is None else total[3 * tile : 3 * tile + 3]
            out += product([tens[h, n, c, rows, :] for c in range(4)], v, part)
        return tuple(out)

    def opened(h, first, tall):
        return tuple(
            acc[h, a, pl.ds(pl.multiple_of(first + 8 * tile, 8), 8), :]
            for tile in range(tall // 8)
            for a in range(3)
        )

    def closed(h, first, total):
        for tile in range(len(total) // 3):
            for a in range(3):
                acc[h, a, pl.ds(pl.multiple_of(first + 8 * tile, 8), 8), :] = total[3 * tile + a]

    def later_own(k, it, unused):
        h, first = it // TALLS, it % TALLS * TALL
        total = apply(k, h, first, 0, h, None)
        total = apply(k, h, first, 1, 1 - h, total)
        closed(h, first, total)
        return unused

    def later_group(k, group, it, unused):
        h, first = it // TALLS, it % TALLS * TALL
        total = opened(h, first, TALL)
        shared = (8, 8, 0)[group]
        rim, slot = ((10, 10 + h), (19, 20 + 4 * h), (23, 28 + 4 * h))[group]
        base = (2, 11, 0)[group]

        def step(n, at, count, total):
            for c in range(count):
                total = apply(k, h, first, n + c, at + c, total)
            return total

        if shared:
            total = lax.fori_loop(
                0,
                shared // CHUNK,
                lambda c, t: step(base + CHUNK * c, GROUPS[group][0] + CHUNK * c, CHUNK, t),
                total,
            )
        total = step(rim, slot, 1 if group == 0 else 4, total)
        closed(h, first, total)
        return unused

    def image(k):
        for h in range(HOMES):
            for a in range(3):
                column = jnp.sum(acc[h, a], axis=1, keepdims=True)
                row = jnp.sum(jnp.where(eye, column, 0.0), axis=0, keepdims=True)
                v = basis[k, h, a]
                nxt = live[h] * (v * invpol[h] - TOTAL * row) - SHIFT * v
                basis[k + 1, h, a] = nxt
                if k < 2:
                    halo_v[k, h, a] = nxt

    exchange(halo, 0)
    for h in range(HOMES):
        place(h)
        cols = jnp.transpose(staged[h])
        for entry, c in enumerate((0, 1, 2, 3, 7)):
            col = cols[:, c : c + 1]
            if c == 3:
                col = col * (-THOLE_A / LN2 / UNIT**3)
            home[h, entry] = jnp.broadcast_to(col, (CL, CL))
    lax.fori_loop(0, HOMES * BLOCKS, first_own, 0)
    for group in range(3):
        arrived(halo, 0, group)
        for slot in range(GROUPS[group][0], sum(GROUPS[group])):
            place(slot)
        lax.fori_loop(0, HOMES * BLOCKS, functools.partial(first_group, group), 0)
    greet(0, 2)
    image(0)
    for k in range(2):
        exchange(halo_v.at[k], 1 + k)
        lax.fori_loop(0, HOMES * TALLS, functools.partial(later_own, k), 0)
        for group in range(3):
            arrived(halo_v.at[k], 1 + k, group)
            lax.fori_loop(0, HOMES * TALLS, functools.partial(later_group, k, group), 0)
        pl.semaphore_wait(greeted.at[k], 2)
        if k == 0:
            greet(1, 4)
        image(1 + k)

    row = jnp.zeros((1, CL), F32)
    for m in range(6):
        part = jnp.zeros((1, CL), F32)
        for h in range(HOMES):
            for a in range(3):
                part = part + basis[m // 2, h, a] * basis[(m + 1) // 2, h, a]
        row = jnp.where(lane == m, jnp.sum(part, axis=1, keepdims=True), row)

    for s, (stage, buf) in enumerate(zip(groups_of, (red_a, red_b))):
        buf[0] = row
        for i, o in enumerate(stage):
            pltpu.make_async_remote_copy(
                src_ref=buf.at[0],
                dst_ref=buf.at[1 + i],
                send_sem=red_send.at[s],
                recv_sem=red_recv.at[s],
                device_id=device(o),
                device_id_type=MESH,
            ).start()
        region = buf.at[pl.ds(1, len(stage))]
        pltpu.make_async_copy(region, region, red_recv.at[s]).wait()
        parts = [buf[i] for i in range(1 + len(stage))]
        while len(parts) > 1:
            parts = [
                parts[i] + parts[i + 1] if i + 1 < len(parts) else parts[i]
                for i in range(0, len(parts), 2)
            ]
        row = parts[0]

    moment = [
        jnp.sum(jnp.where(lane == m, row, 0.0), axis=1, keepdims=True) for m in range(6)
    ]

    def dot(left, right):
        total = None
        for i, x in enumerate(left):
            for j, y in enumerate(right):
                term = moment[i + j] * (x * y)
                total = term if total is None else total + term
        return total

    one = jnp.ones((1, 1), F32)
    res, direction, dip = [one], [one], []
    norm = moment[0]
    for iteration in range(3):
        applied = [SHIFT * c for c in direction] + [jnp.zeros((1, 1), F32)]
        applied = [
            c if i == 0 else c + direction[i - 1] for i, c in enumerate(applied)
        ]
        step = norm / dot(direction, applied)
        dip = [
            step * c + (dip[i] if i < len(dip) else 0.0) for i, c in enumerate(direction)
        ]
        res = [
            (res[i] if i < len(res) else 0.0) - step * c for i, c in enumerate(applied)
        ]
        if iteration < 2:
            new = dot(res, res)
            ratio = new / norm
            direction = [
                c + (ratio * direction[i] if i < len(direction) else 0.0)
                for i, c in enumerate(res)
            ]
            norm = new
    for h in range(HOMES):
        for a in range(3):
            v = [basis[k, h, a] for k in range(4)]
            out_ref[3 * h + a] = dip[0] * v[0] + dip[1] * v[1] + dip[2] * v[2]
            out_ref[6 + 3 * h + a] = res[0] * v[0] + res[1] * v[1] + res[2] * v[2] + res[3] * v[3]
    sent(halo, 0)
    for k in range(2):
        sent(halo_v.at[k], 1 + k)
    for s, (stage, buf) in enumerate(zip(groups_of, (red_a, red_b))):
        region = buf.at[pl.ds(1, len(stage))]
        pltpu.make_async_copy(region, region, red_send.at[s]).wait()


def solution(mesh):
    sizes = tuple(mesh.shape[a] for a in AXES)
    first, second = stages(sizes)
    vector = jax.ShapeDtypeStruct((2 * HOMES * 3, 1, CL), F32)
    vmem = pl.BlockSpec(memory_space=pltpu.VMEM)
    call = pl.pallas_call(
        functools.partial(kernel, sizes),
        out_shape=vector,
        in_specs=[pl.BlockSpec(memory_space=pl.ANY)] * 5,
        out_specs=vmem,
        scratch_shapes=[
            pltpu.VMEM((14, 1, CL), F32),
            pltpu.VMEM((HOMES, 1, CL), jnp.int32),
            pltpu.SMEM((HOMES,), jnp.int32),
            pltpu.VMEM((36, 8, CL), F32),
            pltpu.VMEM((2, 36, 3, 1, CL), F32),
            pltpu.VMEM((36, 8, CL), F32),
            pltpu.VMEM((HOMES, 5, CL, CL), F32),
            pltpu.VMEM((HOMES, 27, 4, CL, CL), F32),
            pltpu.VMEM((HOMES, 3, CL, CL), F32),
            pltpu.VMEM((4, HOMES, 3, 1, CL), F32),
            pltpu.VMEM((1 + len(first), 1, CL), F32),
            pltpu.VMEM((1 + len(second), 1, CL), F32),
            pltpu.SemaphoreType.DMA((5,)),
            pltpu.SemaphoreType.DMA((3,)),
            pltpu.SemaphoreType.DMA((3, 3)),
            pltpu.SemaphoreType.DMA((2,)),
            pltpu.SemaphoreType.DMA((2,)),
            pltpu.SemaphoreType.REGULAR((2,)),
        ],
        compiler_params=pltpu.CompilerParams(
            collective_id=0, has_side_effects=True, vmem_limit_bytes=32 * 1024 * 1024
        ),
    )

    def shards(positions, polarity, perm_field, groups, occupancy):
        both = call(
            positions.reshape(HOMES * 3, 1, CL),
            polarity.reshape(HOMES, 1, CL),
            perm_field.reshape(HOMES * 3, 1, CL),
            groups.reshape(HOMES, 1, CL),
            occupancy.reshape(HOMES),
        )
        return both[:6].reshape(positions.shape), both[6:].reshape(positions.shape)

    return jax.shard_map(
        shards,
        mesh=mesh,
        in_specs=(
            P("gx", "gy", "gz", None, None),
            P("gx", "gy", "gz", None),
            P("gx", "gy", "gz", None, None),
            P("gx", "gy", "gz", None),
            P("gx", "gy", "gz"),
        ),
        out_specs=(P("gx", "gy", "gz", None, None), P("gx", "gy", "gz", None, None)),
        check_vma=False,
    )
```

```python
import functools
import math

import jax
import jax.numpy as jnp
from jax import lax
from jax.experimental import pallas as pl
from jax.experimental.pallas import tpu as pltpu
from jax.sharding import PartitionSpec as P

CL = 128
CELL_EDGE = 11.0
CUTOFF = 9.0
THOLE_A = 0.39
SHIFT = 1.5
AXES = ("gx", "gy", "gz")
MESH = pl.DeviceIdType.MESH
HOMES = 2
ROWS = 32
BLOCKS = CL // ROWS
TALL = 64
TALLS = CL // TALL
CHUNK = 4
UNIT = 1.0 / CUTOFF
LN2 = math.log(2.0)
TINY = 1e-36
TOTAL = 3.0 * UNIT**3
F32 = jnp.float32

FACES = ((-1, 0), (1, 0), (0, -1), (0, 1))
EDGES = ((-1, -1), (-1, 1), (1, -1), (1, 1))

GROUPS = ((2, 10), (12, 16), (28, 8))


def slot_of(dx, dy, dz):
    if dx == 0:
        return 2 + 2 * FACES.index((dy, dz)) if (dy, dz) in FACES else 12 + 2 * EDGES.index((dy, dz))
    side = 0 if dx < 0 else 1
    if (dy, dz) == (0, 0):
        return 10 + side
    if (dy, dz) in FACES:
        return 20 + 4 * side + FACES.index((dy, dz))
    return 28 + 4 * side + EDGES.index((dy, dz))


OFFSETS = sorted(
    [
        (ex, ey, ez)
        for ex in (-1, 0, 1)
        for ey in (-1, 0, 1)
        for ez in (-1, 0, 1)
        if (ex, ey, ez) != (0, 0, 0)
    ],
    key=lambda o: sum(abs(e) for e in o),
)


def places():
    where = {0: (0, 0, 0), 1: (1, 0, 0)}
    for dx, dy, dz in OFFSETS:
        first = slot_of(dx, dy, dz)
        if dx == 0:
            where[first], where[first + 1] = (0, dy, dz), (1, dy, dz)
        else:
            where[first] = (-1 if dx < 0 else 2, dy, dz)
    return where


PLACES = places()


def stages(sizes):
    def way(o):
        return -sum(min(e, n - e) for e, n in zip(o, sizes))

    first = [(i, j, 0) for i in range(sizes[0]) for j in range(sizes[1]) if (i, j) != (0, 0)]
    second = [(0, 0, k) for k in range(1, sizes[2])]
    return (sorted(first, key=way), sorted(second, key=way))


def kernel(
    sizes,
    pos_ref,
    pol_ref,
    perm_ref,
    grp_ref,
    occ_ref,
    out_ref,
    inbox,
    inbox_grp,
    inbox_occ,
    halo,
    halo_v,
    staged,
    home,
    tens,
    acc,
    spare,
    basis,
    red_a,
    red_b,
    in_sem,
    halo_send,
    halo_recv,
    red_send,
    red_recv,
    greeted,
):
    fetches = [
        pltpu.make_async_copy(pos_ref, inbox.at[pl.ds(0, 6)], in_sem.at[0]),
        pltpu.make_async_copy(perm_ref, inbox.at[pl.ds(6, 6)], in_sem.at[1]),
        pltpu.make_async_copy(pol_ref, inbox.at[pl.ds(12, 2)], in_sem.at[2]),
        pltpu.make_async_copy(grp_ref, inbox_grp, in_sem.at[3]),
        pltpu.make_async_copy(occ_ref, inbox_occ, in_sem.at[4]),
    ]
    for c in fetches:
        c.start()

    here = tuple(lax.axis_index(a) for a in AXES)
    near = [
        {
            o: h if o == 0 else lax.rem(h + (o + n), n)
            for o in (-1, 0, 1)
        }
        for h, n in zip(here, sizes)
    ]

    def device(offset):
        return tuple(
            near[d][o] if o in near[d] else lax.rem(here[d] + o, sizes[d])
            for d, o in enumerate(offset)
        )

    groups_of = stages(sizes)
    barrier = pltpu.get_barrier_semaphore()
    for o in OFFSETS:
        pl.semaphore_signal(barrier, inc=1, device_id=device(o), device_id_type=MESH)

    def greet(step, reach):
        for o in (reach, sizes[2] - reach):
            pl.semaphore_signal(
                greeted.at[step], inc=1, device_id=device((0, 0, o)), device_id_type=MESH
            )

    lane = lax.broadcasted_iota(jnp.int32, (1, CL), 1)
    eye = lax.broadcasted_iota(jnp.int32, (CL, CL), 0) == lax.broadcasted_iota(
        jnp.int32, (CL, CL), 1
    )

    for c in fetches:
        c.wait()
    live = []
    invpol = []
    for h in range(HOMES):
        alive = (lane < inbox_occ[h]).astype(F32)
        live.append(alive)
        pol = inbox[12 + h]
        invpol.append(1.0 / pol)
        for a in range(3):
            halo[h, a : a + 1, :] = inbox[3 * h + a] * UNIT
            vector = alive * inbox[6 + 3 * h + a]
            halo[h, 4 + a : 5 + a, :] = vector
            basis[0, h, a] = vector
        halo[h, 3:4, :] = lax.rsqrt(pol)
        halo[h, 7:8, :] = inbox_grp[h].astype(F32)

    pl.semaphore_wait(barrier, len(OFFSETS))

    def exchange(buf, k):
        for ex, ey, ez in OFFSETS:
            target = slot_of(-ex, -ey, -ez)
            if ex == 0:
                src, dst = buf.at[pl.ds(0, 2)], buf.at[pl.ds(target, 2)]
            else:
                source = 1 if ex == 1 else 0
                src, dst = buf.at[pl.ds(source, 1)], buf.at[pl.ds(target, 1)]
            group = sum(abs(e) for e in (ex, ey, ez)) - 1
            pltpu.make_async_remote_copy(
                src_ref=src,
                dst_ref=dst,
                send_sem=halo_send.at[k],
                recv_sem=halo_recv.at[k, group],
                device_id=device((ex, ey, ez)),
                device_id_type=MESH,
            ).start()

    def arrived(buf, k, group):
        region = buf.at[pl.ds(*GROUPS[group])]
        pltpu.make_async_copy(region, region, halo_recv.at[k, group]).wait()

    def sent(buf, k):
        region = buf.at[pl.ds(2, 34)]
        pltpu.make_async_copy(region, region, halo_send.at[k]).wait()

    def place(slot):
        sub = lax.broadcasted_iota(jnp.int32, (8, CL), 0)
        add = jnp.zeros((8, CL), F32)
        for a in range(3):
            if PLACES[slot][a]:
                add = jnp.where(sub == a, jnp.float32(PLACES[slot][a] * CELL_EDGE * UNIT), add)
        staged[slot] = halo[slot] + add

    def couple_tile(h, first, n, slot, total, own):
        rows = pl.ds(first, 8)
        r = [staged[slot, a : a + 1, :] - home[h, a, rows, :] for a in range(3)]
        d2 = r[0] * r[0] + r[1] * r[1] + r[2] * r[2]
        if own:
            diagonal = lax.broadcasted_iota(jnp.int32, (8, CL), 0) + first
            diagonal = diagonal == lax.broadcasted_iota(jnp.int32, (8, CL), 1)
            d2 = d2 + diagonal.astype(F32)
        inv = lax.rsqrt(d2)
        taper = jnp.maximum(1.0 - d2, 0.0)
        scaled = taper * inv
        g = (scaled * scaled) * inv
        if own:
            g = jnp.where(staged[slot, 7:8, :] != home[h, 4, rows, :], g, 0.0)
        t = (d2 * d2 * inv) * (home[h, 3, rows, :] * staged[slot, 3:4, :])
        ge = g * jnp.exp2(t)
        c3 = g - ge
        z = jnp.maximum(c3 + (LN2 * t) * ge, TINY)
        f = (z * lax.rsqrt(z)) * inv
        m = (f * r[0], f * r[1], f * r[2], c3 * (1.0 / 3.0))
        for c in range(4):
            tens[h, n, c, rows, :] = m[c]
        return product(m, [staged[slot, 4 + a : 5 + a, :] for a in range(3)], total)

    def couple(h, i, n, slot, total, own):
        out = []
        for tile in range(ROWS // 8):
            first = pl.multiple_of(i * ROWS + 8 * tile, 8)
            part = None if total is None else total[3 * tile : 3 * tile + 3]
            out += couple_tile(h, first, n, slot, part, own)
        return tuple(out)

    def product(m, v, total):
        s = m[0] * v[0] + m[1] * v[1] + m[2] * v[2]
        out = [m[a] * s - m[3] * v[a] for a in range(3)]
        return tuple(out if total is None else (t + o for t, o in zip(total, out)))

    def members(group, h):
        if group == 0:
            return [(n, 2 + n - 2) for n in range(2, 10)] + [(10, 10 + h)]
        if group == 1:
            return [(11 + n, 12 + n) for n in range(8)] + [(19 + n, 20 + 4 * h + n) for n in range(4)]
        return [(23 + n, 28 + 4 * h + n) for n in range(4)]

    def first_own(it, unused):
        h, i = it // BLOCKS, it % BLOCKS
        total = couple(h, i, 0, h, None, True)
        total = couple(h, i, 1, 1 - h, total, False)
        closed(h, i * ROWS, total)
        return unused

    def first_group(group, it, unused):
        h, i = it // BLOCKS, it % BLOCKS
        total = opened(h, i * ROWS, ROWS)
        for n, slot in members(group, h):
            total = couple(h, i, n, slot, total, False)
        closed(h, i * ROWS, total)
        return unused

    def apply(k, h, first, n, slot, total):
        v = [halo_v[k, slot, a] for a in range(3)]
        out = []
        for tile in range(TALL // 8):
            rows = pl.ds(pl.multiple_of(first + 8 * tile, 8), 8)
            part = None if total is None else total[3 * tile : 3 * tile + 3]
            out += product([tens[h, n, c, rows, :] for c in range(4)], v, part)
        return tuple(out)

    def opened(h, first, tall):
        return tuple(
            acc[h, a, pl.ds(pl.multiple_of(first + 8 * tile, 8), 8), :]
            for tile in range(tall // 8)
            for a in range(3)
        )

    def closed(h, first, total):
        for tile in range(len(total) // 3):
            for a in range(3):
                acc[h, a, pl.ds(pl.multiple_of(first + 8 * tile, 8), 8), :] = total[3 * tile + a]

    def later_own(k, it, unused):
        h, first = it // TALLS, it % TALLS * TALL
        total = apply(k, h, first, 0, h, None)
        total = apply(k, h, first, 1, 1 - h, total)
        closed(h, first, total)
        return unused

    def later_group(k, group, it, unused):
        h, first = it // TALLS, it % TALLS * TALL
        total = opened(h, first, TALL)
        shared = (8, 8, 0)[group]
        rim, slot = ((10, 10 + h), (19, 20 + 4 * h), (23, 28 + 4 * h))[group]
        base = (2, 11, 0)[group]

        def step(n, at, count, total):
            for c in range(count):
                total = apply(k, h, first, n + c, at + c, total)
            return total

        if shared:
            total = lax.fori_loop(
                0,
                shared // CHUNK,
                lambda c, t: step(base + CHUNK * c, GROUPS[group][0] + CHUNK * c, CHUNK, t),
                total,
            )
        total = step(rim, slot, 1 if group == 0 else 4, total)
        closed(h, first, total)
        return unused

    def half_own(k, it, unused):
        h, first = it // TALLS, it % TALLS * TALL
        total = apply(k, h, first, 0, h, None)
        total = apply(k, h, first, 1, 1 - h, total)
        total = tuple(0.5 * t for t in total)
        closed(h, first, total)
        for tile in range(len(total) // 3):
            for a in range(3):
                spare[h, a, pl.ds(pl.multiple_of(first + 8 * tile, 8), 8), :] = total[3 * tile + a]
        return unused

    def half_group(k, cells, it, unused):
        h, first = it // TALLS, it % TALLS * TALL
        total = opened(h, first, TALL)
        for n, slot in cells:
            total = apply(k, h, first, n, slot, total)
        closed(h, first, total)
        return unused

    def half_rim(k, group, h, i, unused):
        total = opened(h, i * TALL, TALL)
        n, slot, count = ((10, 10 + h, 1), (19, 20 + 4 * h, 4), (23, 28 + 4 * h, 4))[group]
        for c in range(count):
            total = apply(k, h, i * TALL, n + c, slot + c, total)
        closed(h, i * TALL, total)
        return unused

    def half(k, part, group):
        cells = (
            ([(n, n) for n in (4, 5, 8, 9)], [(n - 1, n) for n in range(16, 20)]),
            ([(n, n) for n in (2, 3, 6, 7)], [(n - 1, n) for n in range(12, 16)]),
        )[part]
        if group < 2:
            lax.fori_loop(
                0, HOMES * TALLS, functools.partial(half_group, k, cells[group]), 0
            )
        lax.fori_loop(0, TALLS, functools.partial(half_rim, k, group, 1 - part), 0)

    def image(k):
        for h in range(HOMES):
            for a in range(3):
                column = jnp.sum(acc[h, a], axis=1, keepdims=True)
                row = jnp.sum(jnp.where(eye, column, 0.0), axis=0, keepdims=True)
                v = basis[k, h, a]
                nxt = live[h] * (v * invpol[h] - TOTAL * row) - SHIFT * v
                basis[k + 1, h, a] = nxt
                if k < 2:
                    halo_v[k, h, a] = nxt

    exchange(halo, 0)
    for h in range(HOMES):
        place(h)
        cols = jnp.transpose(staged[h])
        for entry, c in enumerate((0, 1, 2, 3, 7)):
            col = cols[:, c : c + 1]
            if c == 3:
                col = col * (-THOLE_A / LN2 / UNIT**3)
            home[h, entry] = jnp.broadcast_to(col, (CL, CL))
    lax.fori_loop(0, HOMES * BLOCKS, first_own, 0)
    for group in range(3):
        arrived(halo, 0, group)
        for slot in range(GROUPS[group][0], sum(GROUPS[group])):
            place(slot)
        lax.fori_loop(0, HOMES * BLOCKS, functools.partial(first_group, group), 0)
    greet(0, 2)
    image(0)
    exchange(halo_v.at[0], 1)
    lax.fori_loop(0, HOMES * TALLS, functools.partial(later_own, 0), 0)
    for group in range(3):
        arrived(halo_v.at[0], 1, group)
        lax.fori_loop(0, HOMES * TALLS, functools.partial(later_group, 0, group), 0)
    pl.semaphore_wait(greeted.at[0], 2)
    greet(1, 4)
    image(1)
    exchange(halo_v.at[1], 2)
    vectors = [[basis[2, h, a] for a in range(3)] for h in range(HOMES)]
    filler = [jnp.zeros((1, CL), F32)] * 2
    cols = jnp.transpose(jnp.concatenate(vectors[0] + vectors[1] + filler, axis=0))
    for h in range(HOMES):
        for a in range(3):
            home[h, a] = jnp.broadcast_to(cols[:, 3 * h + a : 3 * h + a + 1], (CL, CL))
    lax.fori_loop(0, HOMES * TALLS, functools.partial(half_own, 1), 0)

    row = jnp.zeros((1, CL), F32)
    for m in range(5):
        part = jnp.zeros((1, CL), F32)
        for h in range(HOMES):
            for a in range(3):
                part = part + basis[m // 2, h, a] * basis[(m + 1) // 2, h, a]
        row = jnp.where(lane == m, jnp.sum(part, axis=1, keepdims=True), row)
    part = jnp.zeros((1, CL), F32)
    for h in range(HOMES):
        for v in vectors[h]:
            part = part + v * v * (live[h] * invpol[h] - SHIFT)
    for group in range(3):
        arrived(halo_v.at[1], 2, group)
        half(1, 0, group)
    inner = jnp.zeros((CL, CL), F32)
    for h in range(HOMES):
        for a in range(3):
            inner = inner + home[h, a] * acc[h, a]
    part = part - (2.0 * TOTAL) * jnp.sum(inner, axis=0, keepdims=True)
    row = jnp.where(lane == 5, jnp.sum(part, axis=1, keepdims=True), row)

    pl.semaphore_wait(greeted.at[1], 2)
    for s, (stage, buf) in enumerate(zip(groups_of, (red_a, red_b))):
        buf[0] = row
        for i, o in enumerate(stage):
            pltpu.make_async_remote_copy(
                src_ref=buf.at[0],
                dst_ref=buf.at[1 + i],
                send_sem=red_send.at[s],
                recv_sem=red_recv.at[s],
                device_id=device(o),
                device_id_type=MESH,
            ).start()
        if s == 0:
            for h in range(HOMES):
                for a in range(3):
                    acc[h, a] = acc[h, a] + spare[h, a]
            for group in range(3):
                half(1, 1, group)
            image(2)
        region = buf.at[pl.ds(1, len(stage))]
        pltpu.make_async_copy(region, region, red_recv.at[s]).wait()
        parts = [buf[i] for i in range(1 + len(stage))]
        while len(parts) > 1:
            parts = [
                parts[i] + parts[i + 1] if i + 1 < len(parts) else parts[i]
                for i in range(0, len(parts), 2)
            ]
        row = parts[0]

    moment = [
        jnp.sum(jnp.where(lane == m, row, 0.0), axis=1, keepdims=True) for m in range(6)
    ]

    def dot(left, right):
        total = None
        for i, x in enumerate(left):
            for j, y in enumerate(right):
                term = moment[i + j] * (x * y)
                total = term if total is None else total + term
        return total

    one = jnp.ones((1, 1), F32)
    res, direction, dip = [one], [one], []
    norm = moment[0]
    for iteration in range(3):
        applied = [SHIFT * c for c in direction] + [jnp.zeros((1, 1), F32)]
        applied = [
            c if i == 0 else c + direction[i - 1] for i, c in enumerate(applied)
        ]
        step = norm / dot(direction, applied)
        dip = [
            step * c + (dip[i] if i < len(dip) else 0.0) for i, c in enumerate(direction)
        ]
        res = [
            (res[i] if i < len(res) else 0.0) - step * c for i, c in enumerate(applied)
        ]
        if iteration < 2:
            new = dot(res, res)
            ratio = new / norm
            direction = [
                c + (ratio * direction[i] if i < len(direction) else 0.0)
                for i, c in enumerate(res)
            ]
            norm = new
    for h in range(HOMES):
        for a in range(3):
            v = [basis[k, h, a] for k in range(4)]
            out_ref[3 * h + a] = dip[0] * v[0] + dip[1] * v[1] + dip[2] * v[2]
            out_ref[6 + 3 * h + a] = res[0] * v[0] + res[1] * v[1] + res[2] * v[2] + res[3] * v[3]
    sent(halo, 0)
    for k in range(2):
        sent(halo_v.at[k], 1 + k)
    for s, (stage, buf) in enumerate(zip(groups_of, (red_a, red_b))):
        region = buf.at[pl.ds(1, len(stage))]
        pltpu.make_async_copy(region, region, red_send.at[s]).wait()


def solution(mesh):
    sizes = tuple(mesh.shape[a] for a in AXES)
    first, second = stages(sizes)
    vector = jax.ShapeDtypeStruct((2 * HOMES * 3, 1, CL), F32)
    vmem = pl.BlockSpec(memory_space=pltpu.VMEM)
    call = pl.pallas_call(
        functools.partial(kernel, sizes),
        out_shape=vector,
        in_specs=[pl.BlockSpec(memory_space=pl.ANY)] * 5,
        out_specs=vmem,
        scratch_shapes=[
            pltpu.VMEM((14, 1, CL), F32),
            pltpu.VMEM((HOMES, 1, CL), jnp.int32),
            pltpu.SMEM((HOMES,), jnp.int32),
            pltpu.VMEM((36, 8, CL), F32),
            pltpu.VMEM((2, 36, 3, 1, CL), F32),
            pltpu.VMEM((36, 8, CL), F32),
            pltpu.VMEM((HOMES, 5, CL, CL), F32),
            pltpu.VMEM((HOMES, 27, 4, CL, CL), F32),
            pltpu.VMEM((HOMES, 3, CL, CL), F32),
            pltpu.VMEM((HOMES, 3, CL, CL), F32),
            pltpu.VMEM((4, HOMES, 3, 1, CL), F32),
            pltpu.VMEM((1 + len(first), 1, CL), F32),
            pltpu.VMEM((1 + len(second), 1, CL), F32),
            pltpu.SemaphoreType.DMA((5,)),
            pltpu.SemaphoreType.DMA((3,)),
            pltpu.SemaphoreType.DMA((3, 3)),
            pltpu.SemaphoreType.DMA((2,)),
            pltpu.SemaphoreType.DMA((2,)),
            pltpu.SemaphoreType.REGULAR((2,)),
        ],
        compiler_params=pltpu.CompilerParams(
            collective_id=0, has_side_effects=True, vmem_limit_bytes=32 * 1024 * 1024
        ),
    )

    def shards(positions, polarity, perm_field, groups, occupancy):
        both = call(
            positions.reshape(HOMES * 3, 1, CL),
            polarity.reshape(HOMES, 1, CL),
            perm_field.reshape(HOMES * 3, 1, CL),
            groups.reshape(HOMES, 1, CL),
            occupancy.reshape(HOMES),
        )
        return both[:6].reshape(positions.shape), both[6:].reshape(positions.shape)

    return jax.shard_map(
        shards,
        mesh=mesh,
        in_specs=(
            P("gx", "gy", "gz", None, None),
            P("gx", "gy", "gz", None),
            P("gx", "gy", "gz", None, None),
            P("gx", "gy", "gz", None),
            P("gx", "gy", "gz"),
        ),
        out_specs=(P("gx", "gy", "gz", None, None), P("gx", "gy", "gz", None, None)),
        check_vma=False,
    )
```

```python
import functools
import math

import jax
import jax.numpy as jnp
from jax import lax
from jax.experimental import pallas as pl
from jax.experimental.pallas import tpu as pltpu
from jax.sharding import PartitionSpec as P

CL = 128
CELL_EDGE = 11.0
CUTOFF = 9.0
THOLE_A = 0.39
SHIFT = 1.5
AXES = ("gx", "gy", "gz")
MESH = pl.DeviceIdType.MESH
HOMES = 2
ROWS = 32
BLOCKS = CL // ROWS
TALL = 64
TALLS = CL // TALL
CHUNK = 4
UNIT = 1.0 / CUTOFF
LN2 = math.log(2.0)
TINY = 1e-36
TOTAL = 3.0 * UNIT**3
F32 = jnp.float32

FACES = ((-1, 0), (1, 0), (0, -1), (0, 1))
EDGES = ((-1, -1), (-1, 1), (1, -1), (1, 1))

GROUPS = ((2, 10), (12, 16), (28, 8))


def slot_of(dx, dy, dz):
    if dx == 0:
        return 2 + 2 * FACES.index((dy, dz)) if (dy, dz) in FACES else 12 + 2 * EDGES.index((dy, dz))
    side = 0 if dx < 0 else 1
    if (dy, dz) == (0, 0):
        return 10 + side
    if (dy, dz) in FACES:
        return 20 + 4 * side + FACES.index((dy, dz))
    return 28 + 4 * side + EDGES.index((dy, dz))


OFFSETS = sorted(
    [
        (ex, ey, ez)
        for ex in (-1, 0, 1)
        for ey in (-1, 0, 1)
        for ez in (-1, 0, 1)
        if (ex, ey, ez) != (0, 0, 0)
    ],
    key=lambda o: sum(abs(e) for e in o),
)


def places():
    where = {0: (0, 0, 0), 1: (1, 0, 0)}
    for dx, dy, dz in OFFSETS:
        first = slot_of(dx, dy, dz)
        if dx == 0:
            where[first], where[first + 1] = (0, dy, dz), (1, dy, dz)
        else:
            where[first] = (-1 if dx < 0 else 2, dy, dz)
    return where


PLACES = places()


def stages(sizes):
    def way(o):
        return -sum(min(e, n - e) for e, n in zip(o, sizes))

    first = [(i, j, 0) for i in range(sizes[0]) for j in range(sizes[1]) if (i, j) != (0, 0)]
    second = [(0, 0, k) for k in range(1, sizes[2])]
    return (sorted(first, key=way), sorted(second, key=way))


def kernel(
    sizes,
    pos_ref,
    pol_ref,
    perm_ref,
    grp_ref,
    occ_ref,
    out_ref,
    inbox,
    inbox_grp,
    inbox_occ,
    halo,
    halo_v,
    staged,
    home,
    tens,
    acc,
    spare,
    basis,
    red_a,
    red_b,
    in_sem,
    halo_send,
    halo_recv,
    red_send,
    red_recv,
    greeted,
):
    fetches = [
        pltpu.make_async_copy(pos_ref, inbox.at[pl.ds(0, 6)], in_sem.at[0]),
        pltpu.make_async_copy(perm_ref, inbox.at[pl.ds(6, 6)], in_sem.at[1]),
        pltpu.make_async_copy(pol_ref, inbox.at[pl.ds(12, 2)], in_sem.at[2]),
        pltpu.make_async_copy(grp_ref, inbox_grp, in_sem.at[3]),
        pltpu.make_async_copy(occ_ref, inbox_occ, in_sem.at[4]),
    ]

    here = tuple(lax.axis_index(a) for a in AXES)
    near = [
        {
            o: h if o == 0 else lax.rem(h + (o + n), n)
            for o in (-1, 0, 1)
        }
        for h, n in zip(here, sizes)
    ]

    def device(offset):
        return tuple(
            near[d][o] if o in near[d] else lax.rem(here[d] + o, sizes[d])
            for d, o in enumerate(offset)
        )

    groups_of = stages(sizes)
    barrier = pltpu.get_barrier_semaphore()
    for o in OFFSETS:
        pl.semaphore_signal(barrier, inc=1, device_id=device(o), device_id_type=MESH)
    for c in fetches:
        c.start()

    def greet(step, reach):
        for o in (reach, sizes[2] - reach):
            pl.semaphore_signal(
                greeted.at[step], inc=1, device_id=device((0, 0, o)), device_id_type=MESH
            )

    lane = lax.broadcasted_iota(jnp.int32, (1, CL), 1)
    eye = lax.broadcasted_iota(jnp.int32, (CL, CL), 0) == lax.broadcasted_iota(
        jnp.int32, (CL, CL), 1
    )

    for c in fetches:
        c.wait()
    live = []
    invpol = []
    for h in range(HOMES):
        alive = (lane < inbox_occ[h]).astype(F32)
        live.append(alive)
        pol = inbox[12 + h]
        invpol.append(1.0 / pol)
        for a in range(3):
            halo[h, a : a + 1, :] = inbox[3 * h + a] * UNIT
            vector = alive * inbox[6 + 3 * h + a]
            halo[h, 4 + a : 5 + a, :] = vector
            basis[0, h, a] = vector
        halo[h, 3:4, :] = lax.rsqrt(pol)
        halo[h, 7:8, :] = inbox_grp[h].astype(F32)

    pl.semaphore_wait(barrier, len(OFFSETS))

    def exchange(buf, k):
        for ex, ey, ez in OFFSETS:
            target = slot_of(-ex, -ey, -ez)
            if ex == 0:
                src, dst = buf.at[pl.ds(0, 2)], buf.at[pl.ds(target, 2)]
            else:
                source = 1 if ex == 1 else 0
                src, dst = buf.at[pl.ds(source, 1)], buf.at[pl.ds(target, 1)]
            group = sum(abs(e) for e in (ex, ey, ez)) - 1
            pltpu.make_async_remote_copy(
                src_ref=src,
                dst_ref=dst,
                send_sem=halo_send.at[k],
                recv_sem=halo_recv.at[k, group],
                device_id=device((ex, ey, ez)),
                device_id_type=MESH,
            ).start()

    def arrived(buf, k, group):
        region = buf.at[pl.ds(*GROUPS[group])]
        pltpu.make_async_copy(region, region, halo_recv.at[k, group]).wait()

    def sent(buf, k):
        region = buf.at[pl.ds(2, 34)]
        pltpu.make_async_copy(region, region, halo_send.at[k]).wait()

    def place(slot):
        sub = lax.broadcasted_iota(jnp.int32, (8, CL), 0)
        add = jnp.zeros((8, CL), F32)
        for a in range(3):
            if PLACES[slot][a]:
                add = jnp.where(sub == a, jnp.float32(PLACES[slot][a] * CELL_EDGE * UNIT), add)
        staged[slot] = halo[slot] + add

    def couple_tile(h, first, n, slot, total, own):
        rows = pl.ds(first, 8)
        r = [staged[slot, a : a + 1, :] - home[h, a, rows, :] for a in range(3)]
        d2 = r[0] * r[0] + r[1] * r[1] + r[2] * r[2]
        if own:
            diagonal = lax.broadcasted_iota(jnp.int32, (8, CL), 0) + first
            diagonal = diagonal == lax.broadcasted_iota(jnp.int32, (8, CL), 1)
            d2 = d2 + diagonal.astype(F32)
        inv = lax.rsqrt(d2)
        taper = jnp.maximum(1.0 - d2, 0.0)
        scaled = taper * inv
        g = (scaled * scaled) * inv
        if own:
            g = jnp.where(staged[slot, 7:8, :] != home[h, 4, rows, :], g, 0.0)
        t = (d2 * d2 * inv) * (home[h, 3, rows, :] * staged[slot, 3:4, :])
        ge = g * jnp.exp2(t)
        c3 = g - ge
        z = jnp.maximum(c3 + (LN2 * t) * ge, TINY)
        f = (z * lax.rsqrt(z)) * inv
        m = (f * r[0], f * r[1], f * r[2], c3 * (1.0 / 3.0))
        for c in range(4):
            tens[h, n, c, rows, :] = m[c]
        return product(m, [staged[slot, 4 + a : 5 + a, :] for a in range(3)], total)

    def couple(h, i, n, slot, total, own):
        out = []
        for tile in range(ROWS // 8):
            first = pl.multiple_of(i * ROWS + 8 * tile, 8)
            part = None if total is None else total[3 * tile : 3 * tile + 3]
            out += couple_tile(h, first, n, slot, part, own)
        return tuple(out)

    def product(m, v, total):
        s = m[0] * v[0] + m[1] * v[1] + m[2] * v[2]
        out = [m[a] * s - m[3] * v[a] for a in range(3)]
        return tuple(out if total is None else (t + o for t, o in zip(total, out)))

    def members(group, h):
        if group == 0:
            return [(n, 2 + n - 2) for n in range(2, 10)] + [(10, 10 + h)]
        if group == 1:
            return [(11 + n, 12 + n) for n in range(8)] + [(19 + n, 20 + 4 * h + n) for n in range(4)]
        return [(23 + n, 28 + 4 * h + n) for n in range(4)]

    def first_own(it, unused):
        h, i = it // BLOCKS, it % BLOCKS
        total = couple(h, i, 0, h, None, True)
        total = couple(h, i, 1, 1 - h, total, False)
        closed(h, i * ROWS, total)
        return unused

    def first_group(group, it, unused):
        h, i = it // BLOCKS, it % BLOCKS
        total = opened(h, i * ROWS, ROWS)
        for n, slot in members(group, h):
            total = couple(h, i, n, slot, total, False)
        closed(h, i * ROWS, total)
        return unused

    def apply(k, h, first, n, slot, total):
        v = [halo_v[k, slot, a] for a in range(3)]
        out = []
        for tile in range(TALL // 8):
            rows = pl.ds(pl.multiple_of(first + 8 * tile, 8), 8)
            part = None if total is None else total[3 * tile : 3 * tile + 3]
            out += product([tens[h, n, c, rows, :] for c in range(4)], v, part)
        return tuple(out)

    def opened(h, first, tall):
        return tuple(
            acc[h, a, pl.ds(pl.multiple_of(first + 8 * tile, 8), 8), :]
            for tile in range(tall // 8)
            for a in range(3)
        )

    def closed(h, first, total):
        for tile in range(len(total) // 3):
            for a in range(3):
                acc[h, a, pl.ds(pl.multiple_of(first + 8 * tile, 8), 8), :] = total[3 * tile + a]

    def later_own(k, it, unused):
        h, first = it // TALLS, it % TALLS * TALL
        total = apply(k, h, first, 0, h, None)
        total = apply(k, h, first, 1, 1 - h, total)
        closed(h, first, total)
        return unused

    def later_group(k, group, it, unused):
        h, first = it // TALLS, it % TALLS * TALL
        total = opened(h, first, TALL)
        shared = (8, 8, 0)[group]
        rim, slot = ((10, 10 + h), (19, 20 + 4 * h), (23, 28 + 4 * h))[group]
        base = (2, 11, 0)[group]

        def step(n, at, count, total):
            for c in range(count):
                total = apply(k, h, first, n + c, at + c, total)
            return total

        if shared:
            total = lax.fori_loop(
                0,
                shared // CHUNK,
                lambda c, t: step(base + CHUNK * c, GROUPS[group][0] + CHUNK * c, CHUNK, t),
                total,
            )
        total = step(rim, slot, 1 if group == 0 else 4, total)
        closed(h, first, total)
        return unused

    def half_own(k, it, unused):
        h, first = it // TALLS, it % TALLS * TALL
        total = apply(k, h, first, 0, h, None)
        total = apply(k, h, first, 1, 1 - h, total)
        total = tuple(0.5 * t for t in total)
        closed(h, first, total)
        for tile in range(len(total) // 3):
            for a in range(3):
                spare[h, a, pl.ds(pl.multiple_of(first + 8 * tile, 8), 8), :] = total[3 * tile + a]
        return unused

    def half_group(k, cells, it, unused):
        h, first = it // TALLS, it % TALLS * TALL
        total = opened(h, first, TALL)
        for n, slot in cells:
            total = apply(k, h, first, n, slot, total)
        closed(h, first, total)
        return unused

    def half_rim(k, group, h, i, unused):
        total = opened(h, i * TALL, TALL)
        n, slot, count = ((10, 10 + h, 1), (19, 20 + 4 * h, 4), (23, 28 + 4 * h, 4))[group]
        for c in range(count):
            total = apply(k, h, i * TALL, n + c, slot + c, total)
        closed(h, i * TALL, total)
        return unused

    def half(k, part, group):
        cells = (
            ([(n, n) for n in (4, 5, 8, 9)], [(n - 1, n) for n in range(16, 20)]),
            ([(n, n) for n in (2, 3, 6, 7)], [(n - 1, n) for n in range(12, 16)]),
        )[part]
        if group < 2:
            lax.fori_loop(
                0, HOMES * TALLS, functools.partial(half_group, k, cells[group]), 0
            )
        lax.fori_loop(0, TALLS, functools.partial(half_rim, k, group, 1 - part), 0)

    def image(k):
        for h in range(HOMES):
            for a in range(3):
                column = jnp.sum(acc[h, a], axis=1, keepdims=True)
                row = jnp.sum(jnp.where(eye, column, 0.0), axis=0, keepdims=True)
                v = basis[k, h, a]
                nxt = live[h] * (v * invpol[h] - TOTAL * row) - SHIFT * v
                basis[k + 1, h, a] = nxt
                if k < 2:
                    halo_v[k, h, a] = nxt

    exchange(halo, 0)
    for h in range(HOMES):
        place(h)
        cols = jnp.transpose(staged[h])
        for entry, c in enumerate((0, 1, 2, 3, 7)):
            col = cols[:, c : c + 1]
            if c == 3:
                col = col * (-THOLE_A / LN2 / UNIT**3)
            home[h, entry] = jnp.broadcast_to(col, (CL, CL))
    lax.fori_loop(0, HOMES * BLOCKS, first_own, 0)
    for group in range(3):
        arrived(halo, 0, group)
        for slot in range(GROUPS[group][0], sum(GROUPS[group])):
            place(slot)
        lax.fori_loop(0, HOMES * BLOCKS, functools.partial(first_group, group), 0)
    greet(0, 2)
    image(0)
    exchange(halo_v.at[0], 1)
    lax.fori_loop(0, HOMES * TALLS, functools.partial(later_own, 0), 0)
    for group in range(3):
        arrived(halo_v.at[0], 1, group)
        lax.fori_loop(0, HOMES * TALLS, functools.partial(later_group, 0, group), 0)
    pl.semaphore_wait(greeted.at[0], 2)
    greet(1, 4)
    image(1)
    exchange(halo_v.at[1], 2)
    vectors = [[basis[2, h, a] for a in range(3)] for h in range(HOMES)]
    filler = [jnp.zeros((1, CL), F32)] * 2
    cols = jnp.transpose(jnp.concatenate(vectors[0] + vectors[1] + filler, axis=0))
    for h in range(HOMES):
        for a in range(3):
            home[h, a] = jnp.broadcast_to(cols[:, 3 * h + a : 3 * h + a + 1], (CL, CL))
    lax.fori_loop(0, HOMES * TALLS, functools.partial(half_own, 1), 0)

    row = jnp.zeros((1, CL), F32)
    for m in range(5):
        part = jnp.zeros((1, CL), F32)
        for h in range(HOMES):
            for a in range(3):
                part = part + basis[m // 2, h, a] * basis[(m + 1) // 2, h, a]
        row = jnp.where(lane == m, jnp.sum(part, axis=1, keepdims=True), row)
    part = jnp.zeros((1, CL), F32)
    for h in range(HOMES):
        for v in vectors[h]:
            part = part + v * v * (live[h] * invpol[h] - SHIFT)
    for group in range(3):
        arrived(halo_v.at[1], 2, group)
        half(1, 0, group)
    inner = jnp.zeros((CL, CL), F32)
    for h in range(HOMES):
        for a in range(3):
            inner = inner + home[h, a] * acc[h, a]
    part = part - (2.0 * TOTAL) * jnp.sum(inner, axis=0, keepdims=True)
    row = jnp.where(lane == 5, jnp.sum(part, axis=1, keepdims=True), row)

    pl.semaphore_wait(greeted.at[1], 2)
    for s, (stage, buf) in enumerate(zip(groups_of, (red_a, red_b))):
        buf[0] = row
        for i, o in enumerate(stage):
            pltpu.make_async_remote_copy(
                src_ref=buf.at[0],
                dst_ref=buf.at[1 + i],
                send_sem=red_send.at[s],
                recv_sem=red_recv.at[s],
                device_id=device(o),
                device_id_type=MESH,
            ).start()
        if s == 0:
            for h in range(HOMES):
                for a in range(3):
                    acc[h, a] = acc[h, a] + spare[h, a]
            for group in range(3):
                half(1, 1, group)
            image(2)
        region = buf.at[pl.ds(1, len(stage))]
        pltpu.make_async_copy(region, region, red_recv.at[s]).wait()
        parts = [buf[i] for i in range(1 + len(stage))]
        while len(parts) > 1:
            parts = [
                parts[i] + parts[i + 1] if i + 1 < len(parts) else parts[i]
                for i in range(0, len(parts), 2)
            ]
        row = parts[0]

    moment = [
        jnp.sum(jnp.where(lane == m, row, 0.0), axis=1, keepdims=True) for m in range(6)
    ]

    def dot(left, right):
        total = None
        for i, x in enumerate(left):
            for j, y in enumerate(right):
                term = moment[i + j] * (x * y)
                total = term if total is None else total + term
        return total

    one = jnp.ones((1, 1), F32)
    res, direction, dip = [one], [one], []
    norm = moment[0]
    for iteration in range(3):
        applied = [SHIFT * c for c in direction] + [jnp.zeros((1, 1), F32)]
        applied = [
            c if i == 0 else c + direction[i - 1] for i, c in enumerate(applied)
        ]
        step = norm / dot(direction, applied)
        dip = [
            step * c + (dip[i] if i < len(dip) else 0.0) for i, c in enumerate(direction)
        ]
        res = [
            (res[i] if i < len(res) else 0.0) - step * c for i, c in enumerate(applied)
        ]
        if iteration < 2:
            new = dot(res, res)
            ratio = new / norm
            direction = [
                c + (ratio * direction[i] if i < len(direction) else 0.0)
                for i, c in enumerate(res)
            ]
            norm = new
    for h in range(HOMES):
        for a in range(3):
            v = [basis[k, h, a] for k in range(4)]
            out_ref[3 * h + a] = dip[0] * v[0] + dip[1] * v[1] + dip[2] * v[2]
            out_ref[6 + 3 * h + a] = res[0] * v[0] + res[1] * v[1] + res[2] * v[2] + res[3] * v[3]
    sent(halo, 0)
    for k in range(2):
        sent(halo_v.at[k], 1 + k)
    for s, (stage, buf) in enumerate(zip(groups_of, (red_a, red_b))):
        region = buf.at[pl.ds(1, len(stage))]
        pltpu.make_async_copy(region, region, red_send.at[s]).wait()


def solution(mesh):
    sizes = tuple(mesh.shape[a] for a in AXES)
    first, second = stages(sizes)
    vector = jax.ShapeDtypeStruct((2 * HOMES * 3, 1, CL), F32)
    vmem = pl.BlockSpec(memory_space=pltpu.VMEM)
    call = pl.pallas_call(
        functools.partial(kernel, sizes),
        out_shape=vector,
        in_specs=[pl.BlockSpec(memory_space=pl.ANY)] * 5,
        out_specs=vmem,
        scratch_shapes=[
            pltpu.VMEM((14, 1, CL), F32),
            pltpu.VMEM((HOMES, 1, CL), jnp.int32),
            pltpu.SMEM((HOMES,), jnp.int32),
            pltpu.VMEM((36, 8, CL), F32),
            pltpu.VMEM((2, 36, 3, 1, CL), F32),
            pltpu.VMEM((36, 8, CL), F32),
            pltpu.VMEM((HOMES, 5, CL, CL), F32),
            pltpu.VMEM((HOMES, 27, 4, CL, CL), F32),
            pltpu.VMEM((HOMES, 3, CL, CL), F32),
            pltpu.VMEM((HOMES, 3, CL, CL), F32),
            pltpu.VMEM((4, HOMES, 3, 1, CL), F32),
            pltpu.VMEM((1 + len(first), 1, CL), F32),
            pltpu.VMEM((1 + len(second), 1, CL), F32),
            pltpu.SemaphoreType.DMA((5,)),
            pltpu.SemaphoreType.DMA((3,)),
            pltpu.SemaphoreType.DMA((3, 3)),
            pltpu.SemaphoreType.DMA((2,)),
            pltpu.SemaphoreType.DMA((2,)),
            pltpu.SemaphoreType.REGULAR((2,)),
        ],
        compiler_params=pltpu.CompilerParams(
            collective_id=0, has_side_effects=True, vmem_limit_bytes=32 * 1024 * 1024
        ),
    )

    def shards(positions, polarity, perm_field, groups, occupancy):
        inputs = (
            positions.reshape(HOMES * 3, 1, CL),
            polarity.reshape(HOMES, 1, CL),
            perm_field.reshape(HOMES * 3, 1, CL),
            groups.reshape(HOMES, 1, CL),
            occupancy.reshape(HOMES),
        )
        both = call(*[pltpu.with_memory_space_constraint(v, pltpu.HBM) for v in inputs])
        return both[:6].reshape(positions.shape), both[6:].reshape(positions.shape)

    return jax.shard_map(
        shards,
        mesh=mesh,
        in_specs=(
            P("gx", "gy", "gz", None, None),
            P("gx", "gy", "gz", None),
            P("gx", "gy", "gz", None, None),
            P("gx", "gy", "gz", None),
            P("gx", "gy", "gz"),
        ),
        out_specs=(P("gx", "gy", "gz", None, None), P("gx", "gy", "gz", None, None)),
        check_vma=False,
    )
```

```python
import functools
import math

import jax
import jax.numpy as jnp
from jax import lax
from jax.experimental import pallas as pl
from jax.experimental.pallas import tpu as pltpu
from jax.sharding import PartitionSpec as P

CL = 128
CELL_EDGE = 11.0
CUTOFF = 9.0
THOLE_A = 0.39
SHIFT = 1.5
AXES = ("gx", "gy", "gz")
MESH = pl.DeviceIdType.MESH
HOMES = 2
ROWS = 32
BLOCKS = CL // ROWS
TALL = 64
TALLS = CL // TALL
CHUNK = 4
UNIT = 1.0 / CUTOFF
LN2 = math.log(2.0)
TINY = 1e-36
TOTAL = 3.0 * UNIT**3
F32 = jnp.float32

FACES = ((-1, 0), (1, 0), (0, -1), (0, 1))
EDGES = ((-1, -1), (-1, 1), (1, -1), (1, 1))

GROUPS = ((2, 10), (12, 16), (28, 8))


def slot_of(dx, dy, dz):
    if dx == 0:
        return 2 + 2 * FACES.index((dy, dz)) if (dy, dz) in FACES else 12 + 2 * EDGES.index((dy, dz))
    side = 0 if dx < 0 else 1
    if (dy, dz) == (0, 0):
        return 10 + side
    if (dy, dz) in FACES:
        return 20 + 4 * side + FACES.index((dy, dz))
    return 28 + 4 * side + EDGES.index((dy, dz))


OFFSETS = sorted(
    [
        (ex, ey, ez)
        for ex in (-1, 0, 1)
        for ey in (-1, 0, 1)
        for ez in (-1, 0, 1)
        if (ex, ey, ez) != (0, 0, 0)
    ],
    key=lambda o: sum(abs(e) for e in o),
)


def places():
    where = {0: (0, 0, 0), 1: (1, 0, 0)}
    for dx, dy, dz in OFFSETS:
        first = slot_of(dx, dy, dz)
        if dx == 0:
            where[first], where[first + 1] = (0, dy, dz), (1, dy, dz)
        else:
            where[first] = (-1 if dx < 0 else 2, dy, dz)
    return where


PLACES = places()


def stages(sizes):
    def way(o):
        return -sum(min(e, n - e) for e, n in zip(o, sizes))

    first = [(i, j, 0) for i in range(sizes[0]) for j in range(sizes[1]) if (i, j) != (0, 0)]
    second = [(0, 0, k) for k in range(1, sizes[2])]
    return (sorted(first, key=way), sorted(second, key=way))


def kernel(
    sizes,
    pos_ref,
    pol_ref,
    perm_ref,
    grp_ref,
    occ_ref,
    out_ref,
    inbox,
    inbox_grp,
    inbox_occ,
    halo,
    halo_v,
    staged,
    home,
    tens,
    acc,
    spare,
    basis,
    red_a,
    red_b,
    in_sem,
    halo_send,
    halo_recv,
    red_send,
    red_recv,
    greeted,
):
    fetches = [
        pltpu.make_async_copy(pos_ref, inbox.at[pl.ds(0, 6)], in_sem.at[0]),
        pltpu.make_async_copy(perm_ref, inbox.at[pl.ds(6, 6)], in_sem.at[1]),
        pltpu.make_async_copy(pol_ref, inbox.at[pl.ds(12, 2)], in_sem.at[2]),
        pltpu.make_async_copy(grp_ref, inbox_grp, in_sem.at[3]),
        pltpu.make_async_copy(occ_ref, inbox_occ, in_sem.at[4]),
    ]

    here = tuple(lax.axis_index(a) for a in AXES)
    near = [
        {
            o: h if o == 0 else lax.rem(h + (o + n), n)
            for o in (-1, 0, 1)
        }
        for h, n in zip(here, sizes)
    ]

    def device(offset):
        return tuple(
            near[d][o] if o in near[d] else lax.rem(here[d] + o, sizes[d])
            for d, o in enumerate(offset)
        )

    groups_of = stages(sizes)
    barrier = pltpu.get_barrier_semaphore()
    for o in OFFSETS:
        pl.semaphore_signal(barrier, inc=1, device_id=device(o), device_id_type=MESH)
    for c in fetches:
        c.start()

    def greet(step, reach):
        for o in (reach, sizes[2] - reach):
            pl.semaphore_signal(
                greeted.at[step], inc=1, device_id=device((0, 0, o)), device_id_type=MESH
            )

    lane = lax.broadcasted_iota(jnp.int32, (1, CL), 1)
    eye = lax.broadcasted_iota(jnp.int32, (CL, CL), 0) == lax.broadcasted_iota(
        jnp.int32, (CL, CL), 1
    )

    for c in fetches:
        c.wait()
    live = []
    invpol = []
    for h in range(HOMES):
        alive = (lane < inbox_occ[h]).astype(F32)
        live.append(alive)
        pol = inbox[12 + h]
        invpol.append(1.0 / pol)
        for a in range(3):
            halo[h, a : a + 1, :] = inbox[3 * h + a] * UNIT
            vector = alive * inbox[6 + 3 * h + a]
            halo[h, 4 + a : 5 + a, :] = vector
            basis[0, h, a] = vector
        halo[h, 3:4, :] = lax.rsqrt(pol)
        halo[h, 7:8, :] = inbox_grp[h].astype(F32)

    pl.semaphore_wait(barrier, len(OFFSETS))

    def exchange(buf, k):
        for ex, ey, ez in OFFSETS:
            target = slot_of(-ex, -ey, -ez)
            if ex == 0:
                src, dst = buf.at[pl.ds(0, 2)], buf.at[pl.ds(target, 2)]
            else:
                source = 1 if ex == 1 else 0
                src, dst = buf.at[pl.ds(source, 1)], buf.at[pl.ds(target, 1)]
            group = sum(abs(e) for e in (ex, ey, ez)) - 1
            pltpu.make_async_remote_copy(
                src_ref=src,
                dst_ref=dst,
                send_sem=halo_send.at[k],
                recv_sem=halo_recv.at[k, group],
                device_id=device((ex, ey, ez)),
                device_id_type=MESH,
            ).start()

    def arrived(buf, k, group):
        region = buf.at[pl.ds(*GROUPS[group])]
        pltpu.make_async_copy(region, region, halo_recv.at[k, group]).wait()

    def sent(buf, k):
        region = buf.at[pl.ds(2, 34)]
        pltpu.make_async_copy(region, region, halo_send.at[k]).wait()

    def place(slot):
        sub = lax.broadcasted_iota(jnp.int32, (8, CL), 0)
        add = jnp.zeros((8, CL), F32)
        for a in range(3):
            if PLACES[slot][a]:
                add = jnp.where(sub == a, jnp.float32(PLACES[slot][a] * CELL_EDGE * UNIT), add)
        staged[slot] = halo[slot] + add

    def couple_tile(h, first, n, slot, total, own):
        rows = pl.ds(first, 8)
        r = [staged[slot, a : a + 1, :] - home[h, a, rows, :] for a in range(3)]
        d2 = r[0] * r[0] + r[1] * r[1] + r[2] * r[2]
        if own:
            diagonal = lax.broadcasted_iota(jnp.int32, (8, CL), 0) + first
            diagonal = diagonal == lax.broadcasted_iota(jnp.int32, (8, CL), 1)
            d2 = d2 + diagonal.astype(F32)
        inv = lax.rsqrt(d2)
        taper = jnp.maximum(1.0 - d2, 0.0)
        scaled = taper * inv
        g = (scaled * scaled) * inv
        if own:
            g = jnp.where(staged[slot, 7:8, :] != home[h, 4, rows, :], g, 0.0)
        t = (d2 * d2 * inv) * (home[h, 3, rows, :] * staged[slot, 3:4, :])
        ge = g * jnp.exp2(t)
        c3 = g - ge
        z = jnp.maximum(c3 + (LN2 * t) * ge, TINY)
        f = (z * lax.rsqrt(z)) * inv
        m = (f * r[0], f * r[1], f * r[2], c3 * (1.0 / 3.0))
        for c in range(4):
            tens[h, n, c, rows, :] = m[c]
        return product(m, [staged[slot, 4 + a : 5 + a, :] for a in range(3)], total)

    def couple(h, i, n, slot, total, own):
        out = []
        for tile in range(ROWS // 8):
            first = pl.multiple_of(i * ROWS + 8 * tile, 8)
            part = None if total is None else total[3 * tile : 3 * tile + 3]
            out += couple_tile(h, first, n, slot, part, own)
        return tuple(out)

    def product(m, v, total):
        s = m[0] * v[0] + m[1] * v[1] + m[2] * v[2]
        out = [m[a] * s - m[3] * v[a] for a in range(3)]
        return tuple(out if total is None else (t + o for t, o in zip(total, out)))

    def members(group, h):
        if group == 0:
            return [(n, 2 + n - 2) for n in range(2, 10)] + [(10, 10 + h)]
        if group == 1:
            return [(11 + n, 12 + n) for n in range(8)] + [(19 + n, 20 + 4 * h + n) for n in range(4)]
        return [(23 + n, 28 + 4 * h + n) for n in range(4)]

    def first_own(it, unused):
        h, i = it // BLOCKS, it % BLOCKS
        total = couple(h, i, 0, h, None, True)
        total = couple(h, i, 1, 1 - h, total, False)
        closed(h, i * ROWS, total)
        return unused

    def first_group(group, it, unused):
        h, i = it // BLOCKS, it % BLOCKS
        total = opened(h, i * ROWS, ROWS)
        for n, slot in members(group, h):
            total = couple(h, i, n, slot, total, False)
        closed(h, i * ROWS, total)
        return unused

    def apply(k, h, first, n, slot, total):
        v = [halo_v[k, slot, a] for a in range(3)]
        out = []
        for tile in range(TALL // 8):
            rows = pl.ds(pl.multiple_of(first + 8 * tile, 8), 8)
            part = None if total is None else total[3 * tile : 3 * tile + 3]
            out += product([tens[h, n, c, rows, :] for c in range(4)], v, part)
        return tuple(out)

    def opened(h, first, tall):
        return tuple(
            acc[h, a, pl.ds(pl.multiple_of(first + 8 * tile, 8), 8), :]
            for tile in range(tall // 8)
            for a in range(3)
        )

    def closed(h, first, total):
        for tile in range(len(total) // 3):
            for a in range(3):
                acc[h, a, pl.ds(pl.multiple_of(first + 8 * tile, 8), 8), :] = total[3 * tile + a]

    def later_own(k, it, unused):
        h, first = it // TALLS, it % TALLS * TALL
        total = apply(k, h, first, 0, h, None)
        total = apply(k, h, first, 1, 1 - h, total)
        closed(h, first, total)
        return unused

    def later_group(k, group, it, unused):
        h, first = it // TALLS, it % TALLS * TALL
        total = opened(h, first, TALL)
        shared = (8, 8, 0)[group]
        rim, slot = ((10, 10 + h), (19, 20 + 4 * h), (23, 28 + 4 * h))[group]
        base = (2, 11, 0)[group]

        def step(n, at, count, total):
            for c in range(count):
                total = apply(k, h, first, n + c, at + c, total)
            return total

        if shared:
            total = lax.fori_loop(
                0,
                shared // CHUNK,
                lambda c, t: step(base + CHUNK * c, GROUPS[group][0] + CHUNK * c, CHUNK, t),
                total,
            )
        total = step(rim, slot, 1 if group == 0 else 4, total)
        closed(h, first, total)
        return unused

    def half_own(k, it, unused):
        h, first = it // TALLS, it % TALLS * TALL
        total = apply(k, h, first, 0, h, None)
        total = apply(k, h, first, 1, 1 - h, total)
        total = tuple(0.5 * t for t in total)
        closed(h, first, total)
        for tile in range(len(total) // 3):
            for a in range(3):
                spare[h, a, pl.ds(pl.multiple_of(first + 8 * tile, 8), 8), :] = total[3 * tile + a]
        return unused

    def half_group(k, cells, it, unused):
        h, first = it // TALLS, it % TALLS * TALL
        total = opened(h, first, TALL)
        for n, slot in cells:
            total = apply(k, h, first, n, slot, total)
        closed(h, first, total)
        return unused

    def half_rim(k, group, h, i, unused):
        total = opened(h, i * TALL, TALL)
        n, slot, count = ((10, 10 + h, 1), (19, 20 + 4 * h, 4), (23, 28 + 4 * h, 4))[group]
        for c in range(count):
            total = apply(k, h, i * TALL, n + c, slot + c, total)
        closed(h, i * TALL, total)
        return unused

    def half(k, part, group):
        cells = (
            ([(n, n) for n in (4, 5, 8, 9)], [(n - 1, n) for n in range(16, 20)]),
            ([(n, n) for n in (2, 3, 6, 7)], [(n - 1, n) for n in range(12, 16)]),
        )[part]
        if group < 2:
            lax.fori_loop(
                0, HOMES * TALLS, functools.partial(half_group, k, cells[group]), 0
            )
        lax.fori_loop(0, TALLS, functools.partial(half_rim, k, group, 1 - part), 0)

    def image(k):
        for h in range(HOMES):
            for a in range(3):
                column = jnp.sum(acc[h, a], axis=1, keepdims=True)
                row = jnp.sum(jnp.where(eye, column, 0.0), axis=0, keepdims=True)
                v = basis[k, h, a]
                nxt = live[h] * (v * invpol[h] - TOTAL * row) - SHIFT * v
                basis[k + 1, h, a] = nxt
                if k < 2:
                    halo_v[k, h, a] = nxt

    exchange(halo, 0)
    for h in range(HOMES):
        place(h)
        cols = jnp.transpose(staged[h])
        for entry, c in enumerate((0, 1, 2, 3, 7)):
            col = cols[:, c : c + 1]
            if c == 3:
                col = col * (-THOLE_A / LN2 / UNIT**3)
            home[h, entry] = jnp.broadcast_to(col, (CL, CL))
    lax.fori_loop(0, HOMES * BLOCKS, first_own, 0)
    for group in range(3):
        arrived(halo, 0, group)
        for slot in range(GROUPS[group][0], sum(GROUPS[group])):
            place(slot)
        lax.fori_loop(0, HOMES * BLOCKS, functools.partial(first_group, group), 0)
    image(0)
    exchange(halo_v.at[0], 1)
    greet(0, 2)
    lax.fori_loop(0, HOMES * TALLS, functools.partial(later_own, 0), 0)
    for group in range(3):
        arrived(halo_v.at[0], 1, group)
        lax.fori_loop(0, HOMES * TALLS, functools.partial(later_group, 0, group), 0)
    image(1)
    exchange(halo_v.at[1], 2)
    pl.semaphore_wait(greeted.at[0], 2)
    greet(1, 4)
    vectors = [[basis[2, h, a] for a in range(3)] for h in range(HOMES)]
    filler = [jnp.zeros((1, CL), F32)] * 2
    cols = jnp.transpose(jnp.concatenate(vectors[0] + vectors[1] + filler, axis=0))
    for h in range(HOMES):
        for a in range(3):
            home[h, a] = jnp.broadcast_to(cols[:, 3 * h + a : 3 * h + a + 1], (CL, CL))
    lax.fori_loop(0, HOMES * TALLS, functools.partial(half_own, 1), 0)

    row = jnp.zeros((1, CL), F32)
    for m in range(5):
        part = jnp.zeros((1, CL), F32)
        for h in range(HOMES):
            for a in range(3):
                part = part + basis[m // 2, h, a] * basis[(m + 1) // 2, h, a]
        row = jnp.where(lane == m, jnp.sum(part, axis=1, keepdims=True), row)
    part = jnp.zeros((1, CL), F32)
    for h in range(HOMES):
        for v in vectors[h]:
            part = part + v * v * (live[h] * invpol[h] - SHIFT)
    for group in range(3):
        arrived(halo_v.at[1], 2, group)
        half(1, 0, group)
    inner = jnp.zeros((CL, CL), F32)
    for h in range(HOMES):
        for a in range(3):
            inner = inner + home[h, a] * acc[h, a]
    part = part - (2.0 * TOTAL) * jnp.sum(inner, axis=0, keepdims=True)
    row = jnp.where(lane == 5, jnp.sum(part, axis=1, keepdims=True), row)

    pl.semaphore_wait(greeted.at[1], 2)
    for s, (stage, buf) in enumerate(zip(groups_of, (red_a, red_b))):
        buf[0] = row
        for i, o in enumerate(stage):
            pltpu.make_async_remote_copy(
                src_ref=buf.at[0],
                dst_ref=buf.at[1 + i],
                send_sem=red_send.at[s],
                recv_sem=red_recv.at[s],
                device_id=device(o),
                device_id_type=MESH,
            ).start()
        if s == 0:
            for h in range(HOMES):
                for a in range(3):
                    acc[h, a] = acc[h, a] + spare[h, a]
            for group in range(3):
                half(1, 1, group)
            image(2)
        region = buf.at[pl.ds(1, len(stage))]
        pltpu.make_async_copy(region, region, red_recv.at[s]).wait()
        parts = [buf[i] for i in range(1 + len(stage))]
        while len(parts) > 1:
            parts = [
                parts[i] + parts[i + 1] if i + 1 < len(parts) else parts[i]
                for i in range(0, len(parts), 2)
            ]
        row = parts[0]

    moment = [
        jnp.sum(jnp.where(lane == m, row, 0.0), axis=1, keepdims=True) for m in range(6)
    ]

    def dot(left, right):
        total = None
        for i, x in enumerate(left):
            for j, y in enumerate(right):
                term = moment[i + j] * (x * y)
                total = term if total is None else total + term
        return total

    one = jnp.ones((1, 1), F32)
    res, direction, dip = [one], [one], []
    norm = moment[0]
    for iteration in range(3):
        applied = [SHIFT * c for c in direction] + [jnp.zeros((1, 1), F32)]
        applied = [
            c if i == 0 else c + direction[i - 1] for i, c in enumerate(applied)
        ]
        step = norm / dot(direction, applied)
        dip = [
            step * c + (dip[i] if i < len(dip) else 0.0) for i, c in enumerate(direction)
        ]
        res = [
            (res[i] if i < len(res) else 0.0) - step * c for i, c in enumerate(applied)
        ]
        if iteration < 2:
            new = dot(res, res)
            ratio = new / norm
            direction = [
                c + (ratio * direction[i] if i < len(direction) else 0.0)
                for i, c in enumerate(res)
            ]
            norm = new
    for h in range(HOMES):
        for a in range(3):
            v = [basis[k, h, a] for k in range(4)]
            out_ref[3 * h + a] = dip[0] * v[0] + dip[1] * v[1] + dip[2] * v[2]
            out_ref[6 + 3 * h + a] = res[0] * v[0] + res[1] * v[1] + res[2] * v[2] + res[3] * v[3]
    sent(halo, 0)
    for k in range(2):
        sent(halo_v.at[k], 1 + k)
    for s, (stage, buf) in enumerate(zip(groups_of, (red_a, red_b))):
        region = buf.at[pl.ds(1, len(stage))]
        pltpu.make_async_copy(region, region, red_send.at[s]).wait()


def solution(mesh):
    sizes = tuple(mesh.shape[a] for a in AXES)
    first, second = stages(sizes)
    vector = jax.ShapeDtypeStruct((2 * HOMES * 3, 1, CL), F32)
    vmem = pl.BlockSpec(memory_space=pltpu.VMEM)
    call = pl.pallas_call(
        functools.partial(kernel, sizes),
        out_shape=vector,
        in_specs=[pl.BlockSpec(memory_space=pl.ANY)] * 5,
        out_specs=vmem,
        scratch_shapes=[
            pltpu.VMEM((14, 1, CL), F32),
            pltpu.VMEM((HOMES, 1, CL), jnp.int32),
            pltpu.SMEM((HOMES,), jnp.int32),
            pltpu.VMEM((36, 8, CL), F32),
            pltpu.VMEM((2, 36, 3, 1, CL), F32),
            pltpu.VMEM((36, 8, CL), F32),
            pltpu.VMEM((HOMES, 5, CL, CL), F32),
            pltpu.VMEM((HOMES, 27, 4, CL, CL), F32),
            pltpu.VMEM((HOMES, 3, CL, CL), F32),
            pltpu.VMEM((HOMES, 3, CL, CL), F32),
            pltpu.VMEM((4, HOMES, 3, 1, CL), F32),
            pltpu.VMEM((1 + len(first), 1, CL), F32),
            pltpu.VMEM((1 + len(second), 1, CL), F32),
            pltpu.SemaphoreType.DMA((5,)),
            pltpu.SemaphoreType.DMA((3,)),
            pltpu.SemaphoreType.DMA((3, 3)),
            pltpu.SemaphoreType.DMA((2,)),
            pltpu.SemaphoreType.DMA((2,)),
            pltpu.SemaphoreType.REGULAR((2,)),
        ],
        compiler_params=pltpu.CompilerParams(
            collective_id=0, has_side_effects=True, vmem_limit_bytes=32 * 1024 * 1024
        ),
    )

    def shards(positions, polarity, perm_field, groups, occupancy):
        inputs = (
            positions.reshape(HOMES * 3, 1, CL),
            polarity.reshape(HOMES, 1, CL),
            perm_field.reshape(HOMES * 3, 1, CL),
            groups.reshape(HOMES, 1, CL),
            occupancy.reshape(HOMES),
        )
        both = call(*[pltpu.with_memory_space_constraint(v, pltpu.HBM) for v in inputs])
        return both[:6].reshape(positions.shape), both[6:].reshape(positions.shape)

    return jax.shard_map(
        shards,
        mesh=mesh,
        in_specs=(
            P("gx", "gy", "gz", None, None),
            P("gx", "gy", "gz", None),
            P("gx", "gy", "gz", None, None),
            P("gx", "gy", "gz", None),
            P("gx", "gy", "gz"),
        ),
        out_specs=(P("gx", "gy", "gz", None, None), P("gx", "gy", "gz", None, None)),
        check_vma=False,
    )
```
